512 devices in a mesh: prompt: 16 (over x, z_hi), sample: 32 (over y, z_lo, core).
Axes of the slice: x: 4, y: 8, z: 8 (z_hi: 4, z_lo: 2; z = z_hi * 2 + z_lo), core: 2. Of those that a mesh axis runs over, the one named last changes fastest.
Arguments:
- prompt_query: bfloat16 [2048, 4096], P('sample', 'prompt'), may hold values from -120 to 120
- prompt_grad: bfloat16 [2048, 4096], P('sample', 'prompt'), may hold values from -24 to 24
- prompt_out: bfloat16 [2048, 4096], P('sample', 'prompt'), may hold values from -1.75 to 1.75
- prompt_key_codes: bfloat16 [2048, 512], P('prompt'), may hold values from -5 to 5
- prompt_value_codes: bfloat16 [2048, 512], P('prompt'), may hold values from -5 to 5
- key_scales: float32 [64, 4], P('prompt'), may hold values from 0.5 to 2
- value_scales: float32 [64, 4], P('prompt'), may hold values from 0.5 to 2
- response_query: bfloat16 [32, 256, 4096], P('sample', None, 'prompt'), may hold values from -120 to 120
- response_grad: bfloat16 [32, 256, 4096], P('sample', None, 'prompt'), may hold values from -24 to 24
- response_out: bfloat16 [32, 256, 4096], P('sample', None, 'prompt'), may hold values from -1.75 to 1.75
- response_key: bfloat16 [32, 256, 512], P('sample', 'prompt'), may hold values from -6 to 6
- response_value: bfloat16 [32, 256, 512], P('sample', 'prompt'), may hold values from -6 to 6
- lengths: int32 [32], P('sample'), may hold values from 128 to 256, as said below
Outputs:
- prompt_dq: bfloat16 [2048, 4096], P('sample', 'prompt')
- prompt_dk: bfloat16 [2048, 512], P(('prompt', 'sample'))
- prompt_dv: bfloat16 [2048, 512], P(('prompt', 'sample'))
- response_dq: bfloat16 [32, 256, 4096], P('sample', None, 'prompt')
- response_dk: bfloat16 [32, 256, 512], P('sample', 'prompt')
- response_dv: bfloat16 [32, 256, 512], P('sample', 'prompt')
The draws below stay inside these ranges and needn't reach their ends.
Inputs may be any that keep to these rules, and one draw needn't show every extreme that they name: `lengths`: each length is a multiple of 128; some response has length 256.
All inputs are finite; a program needn't handle non-finite values.
Results may differ from the reference program's by a relative error of at most 0.035.
Values may be sent and summed in bfloat16 or wider, within the bound.
A program may use at most 64 MiB of HBM per device.

```python
import math
import jax
import jax.numpy as jnp
from jax import lax

QH = 32
KVH = 4
HD = 128
SBLK = 32
LBLK = 128
RLEN = 256
PLEN = 2048
SAMPLES = 32


def base_codes(key):
    return jnp.clip(jax.random.normal(key, (PLEN, KVH * HD), jnp.float32), -5.0, 5.0)


def draw_prompt_key_codes(key, part):
    codes = base_codes(key)
    result = codes
    return result.astype(jnp.bfloat16)


def draw_prompt_query(key, part):
    key = jax.random.fold_in(key, 12)
    result = jnp.clip(jax.random.normal(key, (PLEN, QH, HD), jnp.float32), -6.0, 6.0)
    return result.reshape(PLEN, QH * HD).astype(jnp.bfloat16)


def draw_response_query(key, part):
    key = jax.random.fold_in(key, 13)
    result = jnp.clip(jax.random.normal(key, (SAMPLES, RLEN, QH, HD), jnp.float32), -6.0, 6.0)
    return result.reshape(SAMPLES, RLEN, QH * HD).astype(jnp.bfloat16)


def draw_lengths(key, part):
    key = jax.random.fold_in(key, 14)
    blocks = jax.random.randint(key, (SAMPLES,), 1, RLEN // LBLK + 1)
    longest = jax.random.randint(jax.random.fold_in(key, 1), (), 0, SAMPLES)
    blocks = jnp.where(jnp.arange(SAMPLES, dtype=jnp.int32) == longest, RLEN // LBLK, blocks)
    return (blocks * LBLK).astype(jnp.int32)


def steps_of(own_key, dims, cuts, smallest, top_value):
    gain = 1.0
    for position, shards_of in cuts:
        heights = jax.random.uniform(jax.random.fold_in(jax.random.fold_in(own_key, 6), position), (shards_of,), jnp.float32, smallest / len(cuts), top_value / len(cuts))
        gain = gain * jnp.repeat(jnp.exp(heights), dims[position] // shards_of).reshape((-1,) + (1,) * (len(dims) - 1 - position))
    return gain


def bell_draw(own_key, extent, deviation, reach, split=(), kind=jnp.bfloat16):
    gain = steps_of(own_key, extent, split, -0.22, 0.18) if split else 1.0
    drawn = jax.random.normal(own_key, extent, jnp.float32) * deviation * gain
    return jnp.minimum(jnp.maximum(drawn, -reach), reach).astype(kind)


def setup_inputs(seed: int = 0) -> dict:
    key_of = jax.random.split(jax.random.key(seed), 14)
    prompt_query = draw_prompt_query(jax.random.fold_in(key_of[13], 71), 0)
    prompt_grad = bell_draw(key_of[1], (PLEN, QH * HD), 4.0, 24.0, ((0, 32), (1, 16)))
    prompt_out = bell_draw(key_of[2], (PLEN, QH * HD), 0.3, 1.75, ((0, 32), (1, 16)))
    prompt_key_codes = draw_prompt_key_codes(jax.random.fold_in(key_of[13], 71), 0)
    prompt_value_codes = bell_draw(key_of[4], (PLEN, KVH * HD), 1.0, 5.0, ((0, 16),))
    key_scales = jnp.clip(jnp.exp(math.log(2.0) - 1.3862944 * jax.random.uniform(key_of[5], (PLEN // SBLK, KVH), jnp.float32) ** steps_of(key_of[5], (PLEN // SBLK, KVH), ((0, 16),), -0.2, 0.2)), 0.5, 2.0)
    value_scales = jnp.clip(jnp.exp(math.log(2.0) - 1.3862944 * jax.random.uniform(key_of[6], (PLEN // SBLK, KVH), jnp.float32) ** steps_of(key_of[6], (PLEN // SBLK, KVH), ((0, 16),), -0.2, 0.2)), 0.5, 2.0)
    response_query = draw_response_query(jax.random.fold_in(key_of[13], 71), 0)
    response_grad = bell_draw(key_of[8], (SAMPLES, RLEN, QH * HD), 4.0, 24.0, ((0, 32), (2, 16)))
    response_out = bell_draw(key_of[9], (SAMPLES, RLEN, QH * HD), 0.3, 1.75, ((0, 32), (2, 16)))
    response_key = bell_draw(key_of[10], (SAMPLES, RLEN, KVH * HD), 1.0, 6.0, ((0, 32), (1, 16)))
    response_value = bell_draw(key_of[11], (SAMPLES, RLEN, KVH * HD), 1.0, 6.0, ((0, 32), (1, 16)))
    lengths = draw_lengths(jax.random.fold_in(key_of[13], 71), 0)
    return {"prompt_query": prompt_query, "prompt_grad": prompt_grad, "prompt_out": prompt_out, "prompt_key_codes": prompt_key_codes, "prompt_value_codes": prompt_value_codes, "key_scales": key_scales, "value_scales": value_scales, "response_query": response_query, "response_grad": response_grad, "response_out": response_out, "response_key": response_key, "response_value": response_value, "lengths": lengths}


NEG_FILL = -1e+30

def dequantize(codes, scales):
    row_total = codes.shape[0]
    blocks = codes.astype(jnp.float32).reshape(row_total // SBLK, SBLK, KVH, HD)
    blocks = blocks * scales.astype(jnp.float32)[:, None, :, None]
    return blocks.astype(jnp.bfloat16).reshape(row_total, KVH, HD)

def softmax_rows(scores, visible):
    masked = jnp.where(visible, scores, NEG_FILL)
    highest = lax.optimization_barrier(jnp.max(masked, axis=-1, keepdims=True))
    powers = jnp.where(visible, jnp.exp(masked - highest), 0.0)
    return powers / lax.optimization_barrier(jnp.sum(powers, axis=-1, keepdims=True))

def reference(prompt_query, prompt_grad, prompt_out, prompt_key_codes, prompt_value_codes, key_scales, value_scales, response_query, response_grad, response_out, response_key, response_value, lengths):
    inv_root = 1.0 / math.sqrt(HD)
    group_size = QH // KVH
    prompt_keys = dequantize(prompt_key_codes, key_scales)
    prompt_values = dequantize(prompt_value_codes, value_scales)
    resp_steps = jnp.arange(RLEN, dtype=jnp.int32)
    live = resp_steps[None, :] < lengths[:, None]
    masked_grad = jnp.where(live[:, :, None], response_grad, jnp.zeros_like(response_grad))
    prompt_delta = lax.optimization_barrier(jnp.sum((prompt_grad.astype(jnp.float32) * prompt_out.astype(jnp.float32)).reshape(PLEN, QH, HD), axis=-1))
    response_delta = lax.optimization_barrier(jnp.sum((masked_grad.astype(jnp.float32) * response_out.astype(jnp.float32)).reshape(SAMPLES, RLEN, QH, HD), axis=-1))
    query_prompt = prompt_query.reshape(PLEN, QH, HD)
    grad_prompt = prompt_grad.reshape(PLEN, QH, HD)
    query_resp = response_query.reshape(SAMPLES, RLEN, QH, HD)
    grad_resp = masked_grad.reshape(SAMPLES, RLEN, QH, HD)
    keys_resp = response_key.reshape(SAMPLES, RLEN, KVH, HD)
    values_resp = response_value.reshape(SAMPLES, RLEN, KVH, HD)
    prompt_steps = jnp.arange(PLEN, dtype=jnp.int32)
    causal_prompt = prompt_steps[:, None] >= prompt_steps[None, :]
    causal_resp = (resp_steps[:, None] >= resp_steps[None, :])[None] & live[:, None, :]
    visible_resp = jnp.concatenate([jnp.ones((SAMPLES, RLEN, PLEN), jnp.bool_), causal_resp], axis=-1)

    def per_head(head):
        kv_head = head // group_size
        head_query = lax.dynamic_index_in_dim(query_prompt, head, 1, False)
        head_grad = lax.dynamic_index_in_dim(grad_prompt, head, 1, False)
        head_delta = lax.dynamic_index_in_dim(prompt_delta, head, 1, False)
        key_head = lax.dynamic_index_in_dim(prompt_keys, kv_head, 1, False)
        value_head = lax.dynamic_index_in_dim(prompt_values, kv_head, 1, False)
        scores = jnp.dot(head_query, key_head.T, preferred_element_type=jnp.float32) * inv_root
        attention = softmax_rows(scores, causal_prompt)
        weights = attention.astype(jnp.bfloat16)
        grad_prob = jnp.dot(head_grad, value_head.T, preferred_element_type=jnp.float32)
        grad_score = (attention * (grad_prob - head_delta[:, None])).astype(jnp.bfloat16)
        dq_prompt = jnp.dot(grad_score, key_head, preferred_element_type=jnp.float32) * inv_root
        dk_prompt = jnp.dot(grad_score.T, head_query, preferred_element_type=jnp.float32) * inv_root
        dv_prompt = jnp.dot(weights.T, head_grad, preferred_element_type=jnp.float32)
        resp_query = lax.dynamic_index_in_dim(query_resp, head, 2, False).astype(jnp.float32)
        resp_grad = lax.dynamic_index_in_dim(grad_resp, head, 2, False).astype(jnp.float32)
        resp_delta = lax.dynamic_index_in_dim(response_delta, head, 2, False)
        resp_keys = lax.dynamic_index_in_dim(keys_resp, kv_head, 2, False).astype(jnp.float32)
        resp_values = lax.dynamic_index_in_dim(values_resp, kv_head, 2, False).astype(jnp.float32)
        key_float = key_head.astype(jnp.float32)
        value_float = value_head.astype(jnp.float32)
        scores_far = jnp.einsum('btd,jd->btj', resp_query, key_float) * inv_root
        scores_near = jnp.einsum('btd,bud->btu', resp_query, resp_keys) * inv_root
        attention_resp = softmax_rows(jnp.concatenate([scores_far, scores_near], axis=-1), visible_resp)
        weights_resp = attention_resp.astype(jnp.bfloat16).astype(jnp.float32)
        grad_far = jnp.einsum('btd,jd->btj', resp_grad, value_float)
        grad_near = jnp.einsum('btd,bud->btu', resp_grad, resp_values)
        grad_all = jnp.concatenate([grad_far, grad_near], axis=-1)
        score_grad = (attention_resp * (grad_all - resp_delta[:, :, None])).astype(jnp.bfloat16).astype(jnp.float32)
        score_far = score_grad[:, :, :PLEN]
        score_near = score_grad[:, :, PLEN:]
        dq_resp = (jnp.einsum('btj,jd->btd', score_far, key_float) + jnp.einsum('btu,bud->btd', score_near, resp_keys)) * inv_root
        dk_from_resp = jnp.einsum('btj,btd->jd', score_far, resp_query) * inv_root
        dv_from_resp = jnp.einsum('btj,btd->jd', weights_resp[:, :, :PLEN], resp_grad)
        dk_resp = jnp.einsum('btu,btd->bud', score_near, resp_query) * inv_root
        dv_resp = jnp.einsum('btu,btd->bud', weights_resp[:, :, PLEN:], resp_grad)
        return (dq_prompt, dq_resp, dk_prompt + dk_from_resp, dv_prompt + dv_from_resp, dk_resp, dv_resp)
    dq_prompt, dq_resp, dk_prompt, dv_prompt, dk_resp, dv_resp = lax.map(per_head, jnp.arange(QH, dtype=jnp.int32))
    prompt_dq = jnp.transpose(dq_prompt, (1, 0, 2)).reshape(PLEN, QH * HD).astype(jnp.bfloat16)
    response_dq = jnp.transpose(dq_resp, (1, 2, 0, 3)).reshape(SAMPLES, RLEN, QH * HD).astype(jnp.bfloat16)
    prompt_dk = jnp.transpose(dk_prompt.reshape(KVH, group_size, PLEN, HD).sum(axis=1), (1, 0, 2)).reshape(PLEN, KVH * HD).astype(jnp.bfloat16)
    prompt_dv = jnp.transpose(dv_prompt.reshape(KVH, group_size, PLEN, HD).sum(axis=1), (1, 0, 2)).reshape(PLEN, KVH * HD).astype(jnp.bfloat16)
    response_dk = jnp.transpose(dk_resp.reshape(KVH, group_size, SAMPLES, RLEN, HD).sum(axis=1), (1, 2, 0, 3)).reshape(SAMPLES, RLEN, KVH * HD).astype(jnp.bfloat16)
    response_dv = jnp.transpose(dv_resp.reshape(KVH, group_size, SAMPLES, RLEN, HD).sum(axis=1), (1, 2, 0, 3)).reshape(SAMPLES, RLEN, KVH * HD).astype(jnp.bfloat16)
    return (prompt_dq, prompt_dk, prompt_dv, response_dq, response_dk, response_dv)
```

```python
import math

import jax
import jax.numpy as jnp
from jax import lax
from jax.experimental import pallas as pl
from jax.experimental.pallas import tpu as pltpu
from jax.sharding import PartitionSpec as P

HD = 128
SBLK = 32
MESH = pl.DeviceIdType.MESH
NEG = -1e30
F32 = jnp.float32
BF = jnp.bfloat16
LOG2E = 1.4426950408889634

NX, NY, NZ, NZH = 4, 8, 8, 4
RESP = 256
PROWS = 64
RL = 2 * RESP
LANES = RL + 2 * PROWS
GROUP = 512


def dot_t(a, b):
    return lax.dot_general(a, b, (((1,), (1,)), ((), ())), preferred_element_type=F32)


def dot_n(a, b):
    return lax.dot_general(a, b, (((1,), (0,)), ((), ())), preferred_element_type=F32)


def dot_l(a, b):
    return lax.dot_general(a, b, (((0,), (0,)), ((), ())), preferred_element_type=F32)


def kernel(
    pq, pg, po, kc, vc, ks, vs, rq, rg, ro, rk, rv, ln,
    o_dq, o_dk, o_dv, o_rdq, o_rdk, o_rdv,
    qm, gm, om, codes, deq, table, rsend, rtab, kr, vr, S, Sr, dqs, dqt,
    gout, r1, ady, adz, ray, raz, bdy, bdz, rby, rbz, fin, rfin, rgs, rgr,
    in_sem, rin_sem, out_sem,
    p_ss, p_rs, q_ss, q_rs, d_ss, d_rs, e_ss, e_rs, ya_ss, ya_rs, za_ss, za_rs,
    yb_ss, yb_rs, zb_ss, zb_rs, f_ss, f_rs, g_ss, g_rs,
):
    p = lax.axis_index("prompt")
    s = lax.axis_index("sample")
    x, zh = p // 4, p % 4
    y, zl, c = s // 4, (s // 2) % 2, s % 2
    z = zh * 2 + zl
    sg = 2 * zl - 1
    inv = 1.0 / math.sqrt(HD)

    def dev(xx, yy, zz, cc):
        return (xx * 4 + zz // 2, yy * 4 + (zz % 2) * 2 + cc)

    def wrap(v, n):
        return lax.rem(v + 2 * n, n)

    def remote(src, dst, ss, rs, to):
        return pltpu.make_async_remote_copy(src, dst, ss, rs, device_id=to, device_id_type=MESH)

    sib = dev(x, y, z, 1 - c)

    bar = pltpu.get_barrier_semaphore()
    partners = []
    for dx in range(NX):
        for dz in range(NZ):
            if dx or dz:
                partners.append(dev(wrap(x + dx, NX), y, wrap(z + dz, NZ), c))
    for dy in range(1, NY):
        partners.append(dev(x, wrap(y + dy, NY), z, c))
    for dx in range(NX):
        for zz in range(2):
            partners.append(dev(wrap(x + dx, NX), y, zh * 2 + zz, 1 - c))
    for to in partners:
        pl.semaphore_signal(bar, inc=1, device_id=to, device_id_type=MESH)

    @pl.when(c == 0)
    def _():
        pltpu.make_async_copy(kc, codes, in_sem.at[12]).start()

    @pl.when(c == 1)
    def _():
        pltpu.make_async_copy(vc, codes, in_sem.at[12]).start()

    rloads = []
    for g in range(NX):
        for i, ref in enumerate((rk, rv)):
            rloads.append(
                pltpu.make_async_copy(
                    ref.at[0, :, pl.ds(g * HD, HD)], rsend.at[g, pl.ds(16 * i, 16)], rin_sem.at[g * 2 + i]
                )
            )
    for cp in rloads:
        cp.start()
    loads = []
    for i, (pref, rref, dst) in enumerate(((pq, rq, qm), (pg, rg, gm), (po, ro, om))):
        for h in range(2):
            loads.append(
                pltpu.make_async_copy(
                    rref.at[0, :, pl.ds(h * HD, HD)], dst.at[pl.ds(h * RESP, RESP)], in_sem.at[i * 4 + h]
                )
            )
            loads.append(
                pltpu.make_async_copy(
                    pref.at[:, pl.ds(h * HD, HD)], dst.at[pl.ds(RL + h * PROWS, PROWS)], in_sem.at[i * 4 + 2 + h]
                )
            )
    for cp in loads:
        cp.start()

    pltpu.make_async_copy(kc, codes, in_sem.at[12]).wait()
    for g in range(NX):
        for b in range(128 // SBLK):
            scale = jnp.where(c == 0, ks[b, g], vs[b, g])
            block = codes[b * SBLK : (b + 1) * SBLK, g * HD : (g + 1) * HD].astype(F32) * scale
            deq[g, b * SBLK : (b + 1) * SBLK, :] = block.astype(BF)
    own_rows = pl.ds(pl.multiple_of(x * 128, 128), 128)
    table[c, zh, own_rows, :] = deq[x]
    for cp in rloads:
        cp.wait()

    pl.semaphore_wait(bar, len(partners))

    psends = []
    for d in (1, 2, 3):
        for dx in range(NX):
            psends.append((wrap(x + dx, NX), wrap(z + sg * d, NZ)))
    for dx in (1, 2, 3):
        psends.append((wrap(x + dx, NX), z))
    pcopies = []
    for i, (xt, zt) in enumerate(psends):
        cp = remote(deq.at[xt], table.at[c, zh, own_rows], p_ss.at[i], p_rs.at[p], dev(xt, y, zt, c))
        cp.start()
        pcopies.append(cp)
    qcopies = []
    for k in range(1, 16):
        pt = wrap(p + k, 16)
        cp = remote(rsend.at[pt // 4], rtab.at[p], q_ss.at[k], q_rs.at[p], (pt, s))
        cp.start()
        qcopies.append(cp)
    rtab[p] = rsend[x]

    groups = [zh, wrap(zh + sg, NZH), wrap(zh - sg, NZH), wrap(zh + 2, NZH)]

    dcopies = []
    for k in range(4):
        zg = groups[k]
        for dx in range(NX):
            xs = wrap(x + dx, NX)
            rows = pl.ds(pl.multiple_of(xs * 128, 128), 128)
            piece = table.at[c, zg, rows]
            if k or dx:
                remote(piece, piece, p_ss.at[0], p_rs.at[xs * 4 + zg], sib).wait_recv()
        cp = remote(table.at[c, zg], table.at[c, zg], d_ss.at[k], d_rs.at[zg], sib)
        cp.start()
        dcopies.append(cp)

    for cp in loads:
        cp.wait()
    length = ln[0]
    live = lax.broadcasted_iota(jnp.int32, (RESP, HD), 0) < length
    for h in range(2):
        block = gm[h * RESP : (h + 1) * RESP, :]
        gm[h * RESP : (h + 1) * RESP, :] = jnp.where(live, block, jnp.zeros_like(block))
    delta = jnp.sum((gm[...].astype(F32) * om[...].astype(F32)).T, axis=0, keepdims=True)

    for k in range(1, 16):
        ps = wrap(p + k, 16)
        remote(rtab.at[ps], rtab.at[ps], q_ss.at[0], q_rs.at[ps], sib).wait_recv()
    for i in range(16):
        kr[i * 16 : (i + 1) * 16, :] = rtab[i, 0:16, :]
        vr[i * 16 : (i + 1) * 16, :] = rtab[i, 16:32, :]

    for k in range(4):
        zg = groups[k]
        other = table.at[1 - c, zg]
        remote(other, other, d_ss.at[0], d_rs.at[zg], sib).wait_recv()

    u = lax.broadcasted_iota(jnp.int32, (RESP, RESP), 0)
    t = lax.broadcasted_iota(jnp.int32, (RESP, RESP), 1)
    near = (u <= t) & (u < length)
    sr = dot_t(kr[...], qm[0:RL, :])
    tops = []
    for h in range(2):
        part = jnp.where(near, sr[:, h * RESP : (h + 1) * RESP], NEG)
        Sr[:, h * RESP : (h + 1) * RESP] = part
        tops.append(jnp.max(part, axis=0, keepdims=True))
    top = jnp.concatenate(tops + [jnp.full((1, 2 * PROWS), NEG, F32)], axis=1)

    def group_of(k):
        step = jnp.where(k == 1, sg, jnp.where(k == 2, -sg, jnp.where(k == 3, 2, 0)))
        return lax.rem(zh + step + 4, 4)

    def scores(k, top):
        zg = group_of(k)
        keys = table[0, zg]
        far = dot_t(keys, qm[0:RL, :])
        S[zg, :, 0:RL] = far
        row = lax.broadcasted_iota(jnp.int32, (GROUP, 2 * PROWS), 0)
        lane = lax.broadcasted_iota(jnp.int32, (GROUP, 2 * PROWS), 1)
        place = (row // 128) * 512 + zg * 128 + row % 128
        own = dot_t(keys, qm[RL:LANES, :])
        own = jnp.where(place <= s * PROWS + lane % PROWS, own, NEG)
        S[zg, :, RL:LANES] = own
        best = jnp.concatenate([jnp.max(far, axis=0, keepdims=True), jnp.max(own, axis=0, keepdims=True)], axis=1)
        return jnp.maximum(top, best)

    top = lax.fori_loop(0, 4, scores, top)

    er = jnp.exp2((Sr[...] - top[:, 0:RL]) * (inv * LOG2E))
    Sr[...] = er
    total = jnp.concatenate([jnp.sum(er, axis=0, keepdims=True), jnp.zeros((1, 2 * PROWS), F32)], axis=1)

    def powers(k, total):
        zg = group_of(k)
        e = jnp.exp2((S[zg] - top) * (inv * LOG2E))
        S[zg] = e
        return total + jnp.sum(e, axis=0, keepdims=True)

    total = lax.fori_loop(0, 4, powers, total)
    rtotal = 1.0 / total

    prob = Sr[...] * rtotal[:, 0:RL]
    dp = dot_t(vr[...], gm[0:RL, :])
    ds = (prob * (dp - delta[:, 0:RL])).astype(BF)
    dqt[:, 0:RL] = dot_l(kr[...], ds)
    dqt[:, RL:LANES] = jnp.zeros((HD, 2 * PROWS), F32)
    dkr = (dot_n(ds, qm[0:RL, :]) * inv).astype(BF)
    dvr = dot_n(prob.astype(BF), gm[0:RL, :]).astype(BF)
    for i in range(16):
        rgs[i, 0:16, :] = dkr[i * 16 : (i + 1) * 16, :]
        rgs[i, 16:32, :] = dvr[i * 16 : (i + 1) * 16, :]
    gcopies = []
    for k in range(1, 16):
        pt = wrap(p + k, 16)
        cp = remote(rgs.at[pt], rgr.at[p], g_ss.at[k], g_rs.at[p], (pt, s))
        cp.start()
        gcopies.append(cp)
    rgr[p] = rgs[p]

    def grads(k, _):
        zg = group_of(k)
        prob = S[zg] * rtotal
        dp = dot_t(table[1, zg], gm[...])
        ds = (prob * (dp - delta)).astype(BF)
        dqt[...] += dot_l(table[0, zg], ds)
        gout[0, zg] = (dot_n(ds, qm[...]) * inv).astype(BF)
        gout[1, zg] = dot_n(prob.astype(BF), gm[...]).astype(BF)
        for kv in range(2):
            for i in range(2):
                rows = pl.ds(pl.multiple_of((2 * i + 1 - c) * 128, 128), 128)
                remote(
                    gout.at[kv, zg, rows],
                    r1.at[kv, zg, pl.ds(i * 128, 128)],
                    e_ss.at[zg, kv * 2 + i],
                    e_rs.at[zg, kv * 2 + i],
                    sib,
                ).start()
        return 0

    lax.fori_loop(0, 4, grads, 0)

    dqs[...] = (dqt[...].T * inv).astype(BF)
    outs = []
    for h in range(2):
        outs.append(
            pltpu.make_async_copy(
                dqs.at[pl.ds(h * RESP, RESP)], o_rdq.at[0, :, pl.ds(h * HD, HD)], out_sem.at[h]
            )
        )
        outs.append(
            pltpu.make_async_copy(
                dqs.at[pl.ds(RL + h * PROWS, PROWS)], o_dq.at[:, pl.ds(h * HD, HD)], out_sem.at[2 + h]
            )
        )
    for cp in outs:
        cp.start()

    for k in range(4):
        zg = groups[k]
        for kv in range(2):
            for i in range(2):
                rows = pl.ds(pl.multiple_of((2 * i + 1 - c) * 128, 128), 128)
                remote(
                    gout.at[kv, zg, rows], r1.at[kv, zg, pl.ds(i * 128, 128)],
                    e_ss.at[zg, kv * 2 + i], e_rs.at[zg, kv * 2 + i], sib,
                ).wait()
    for zg in range(4):
        for i in range(2):
            zt = zg * 2 + i
            keep = pl.ds(pl.multiple_of((2 * i + c) * 128, 128), 128)
            got = pl.ds(i * 128, 128)
            both = gout[0, zg, keep, :].astype(F32) + r1[0, zg, got, :].astype(F32)
            both = both.astype(BF)
            for yy in range(NY):
                ady[yy, zt * 16 : (zt + 1) * 16, :] = both[yy * 16 : (yy + 1) * 16, :]
            both = gout[1, zg, keep, :].astype(F32) + r1[1, zg, got, :].astype(F32)
            adz[zt] = both.astype(BF)

    ycopies, zcopies = [], []
    for d in range(1, 8):
        yt = wrap(y + d, NY)
        cp = remote(ady.at[yt], ray.at[d], ya_ss.at[d], ya_rs.at[d], dev(x, yt, z, c))
        cp.start()
        ycopies.append(cp)
        zt = wrap(z + d, NZ)
        cp = remote(adz.at[zt], raz.at[d], za_ss.at[d], za_rs.at[d], dev(x, y, zt, c))
        cp.start()
        zcopies.append(cp)
    for cp in ycopies:
        cp.wait_recv()
    acc = ady[y].astype(F32)
    for d in range(1, 8):
        acc += ray[d].astype(F32)
    bdy[...] = acc.astype(BF)
    zb, yb = [], []
    for d in range(1, 8):
        zt = wrap(z + d, NZ)
        cp = remote(
            bdy.at[pl.ds(pl.multiple_of(zt * 16, 16), 16)], rbz.at[d], zb_ss.at[d], zb_rs.at[d], dev(x, y, zt, c)
        )
        cp.start()
        zb.append(cp)
    for cp in zcopies:
        cp.wait_recv()
    acc = adz[z].astype(F32)
    for d in range(1, 8):
        acc += raz[d].astype(F32)
    bdz[...] = acc.astype(BF)
    for d in range(1, 8):
        yt = wrap(y + d, NY)
        cp = remote(
            bdz.at[pl.ds(pl.multiple_of(yt * 16, 16), 16)], rby.at[d], yb_ss.at[d], yb_rs.at[d], dev(x, yt, z, c)
        )
        cp.start()
        yb.append(cp)
    for cp in zb:
        cp.wait_recv()
    acc = bdy[pl.ds(pl.multiple_of(z * 16, 16), 16), :].astype(F32)
    for d in range(1, 8):
        acc += rbz[d].astype(F32)
    fin[0:16, :] = acc.astype(BF)
    for cp in yb:
        cp.wait_recv()
    acc = bdz[pl.ds(pl.multiple_of(y * 16, 16), 16), :].astype(F32)
    for d in range(1, 8):
        acc += rby[d].astype(F32)
    fin[16:32, :] = acc.astype(BF)

    xo = 2 * zl + c
    zs, cs = x // 2, x % 2

    def final(i):
        zz, cc = i // 2, i % 2
        same = (xo == x) & (zl == zz) & (c == cc)
        return same, remote(fin, rfin.at[x], f_ss.at[i], f_rs.at[x], dev(xo, y, zh * 2 + zz, cc))

    for i in range(4):
        same, cp = final(i)

        @pl.when(jnp.logical_not(same))
        def _():
            cp.start()

        @pl.when(same)
        def _():
            rfin[x] = fin[...]

    for cp in gcopies:
        cp.wait_send()
    for k in range(1, 16):
        ps = wrap(p + k, 16)
        remote(rgr.at[ps], rgr.at[ps], g_ss.at[0], g_rs.at[ps], sib).wait_recv()
    for g in range(NX):
        acc = rgr[g * 4].astype(F32)
        for i in range(1, 4):
            acc += rgr[g * 4 + i].astype(F32)
        acc = acc.astype(BF)
        o_rdk[0, :, g * HD : (g + 1) * HD] = acc[0:16, :]
        o_rdv[0, :, g * HD : (g + 1) * HD] = acc[16:32, :]

    for xs in range(NX):
        mine = (x == xs) & (zs == zl) & (cs == c)

        @pl.when(jnp.logical_not(mine))
        def _():
            remote(fin, rfin.at[xs], f_ss.at[0], f_rs.at[xs], sib).wait_recv()

    place = zl * 2 + c
    for xs in range(NX):
        tile = rfin[xs].astype(F32)
        for half, out in ((0, o_dk), (16, o_dv)):
            rows = tile[half : half + 4, :]
            for i in range(1, 4):
                rows = jnp.where(place == i, tile[half + 4 * i : half + 4 * i + 4, :], rows)
            out[:, xs * HD : (xs + 1) * HD] = rows.astype(BF)

    for i in range(4):
        same, cp = final(i)

        @pl.when(jnp.logical_not(same))
        def _():
            cp.wait_send()

    for cp in pcopies + qcopies + dcopies + ycopies + zcopies + zb + yb:
        cp.wait_send()
    for cp in outs:
        cp.wait()


def shards(*args):
    hbm = pl.BlockSpec(memory_space=pl.ANY)
    smem = pl.BlockSpec(memory_space=pltpu.SMEM)
    vmem = pl.BlockSpec(memory_space=pltpu.VMEM)
    dma = pltpu.SemaphoreType.DMA
    shape = jax.ShapeDtypeStruct
    return pl.pallas_call(
        kernel,
        out_shape=(
            shape((PROWS, 256), BF),
            shape((4, 512), BF),
            shape((4, 512), BF),
            shape((1, RESP, 256), BF),
            shape((1, 16, 512), BF),
            shape((1, 16, 512), BF),
        ),
        in_specs=[hbm] * 5 + [smem] * 2 + [hbm] * 5 + [smem],
        out_specs=(hbm, vmem, vmem, hbm, vmem, vmem),
        scratch_shapes=[
            pltpu.VMEM((LANES, HD), BF),
            pltpu.VMEM((LANES, HD), BF),
            pltpu.VMEM((LANES, HD), BF),
            pltpu.VMEM((128, 512), BF),
            pltpu.VMEM((4, 128, HD), BF),
            pltpu.VMEM((2, 4, GROUP, HD), BF),
            pltpu.VMEM((4, 32, HD), BF),
            pltpu.VMEM((16, 32, HD), BF),
            pltpu.VMEM((RESP, HD), BF),
            pltpu.VMEM((RESP, HD), BF),
            pltpu.VMEM((4, GROUP, LANES), F32),
            pltpu.VMEM((RESP, RL), F32),
            pltpu.VMEM((LANES, HD), BF),
            pltpu.VMEM((HD, LANES), F32),
            pltpu.VMEM((2, 4, GROUP, HD), BF),
            pltpu.VMEM((2, 4, 256, HD), BF),
            pltpu.VMEM((8, 128, HD), BF),
            pltpu.VMEM((8, 128, HD), BF),
            pltpu.VMEM((8, 128, HD), BF),
            pltpu.VMEM((8, 128, HD), BF),
            pltpu.VMEM((128, HD), BF),
            pltpu.VMEM((128, HD), BF),
            pltpu.VMEM((8, 16, HD), BF),
            pltpu.VMEM((8, 16, HD), BF),
            pltpu.VMEM((32, HD), BF),
            pltpu.VMEM((4, 32, HD), BF),
            pltpu.VMEM((16, 32, HD), BF),
            pltpu.VMEM((16, 32, HD), BF),
            dma((13,)),
            dma((8,)),
            dma((4,)),
            dma((15,)),
            dma((16,)),
            dma((16,)),
            dma((16,)),
            dma((4,)),
            dma((4,)),
            dma((4, 4)),
            dma((4, 4)),
        ]
        + [dma((8,))] * 8
        + [dma((4,)), dma((4,)), dma((16,)), dma((16,))],
        compiler_params=pltpu.CompilerParams(
            collective_id=0, has_side_effects=True, vmem_limit_bytes=60 * 1024 * 1024
        ),
        name="attention_backward",
    )(*args)


def solution(mesh):
    wide = P("sample", "prompt")
    block = P("prompt", None)
    resp = P("sample", None, "prompt")
    near = P("sample", "prompt", None)
    owned = P(("prompt", "sample"), None)
    return jax.shard_map(
        shards,
        mesh=mesh,
        in_specs=(wide, wide, wide, block, block, block, block, resp, resp, resp, near, near, P("sample")),
        out_specs=(wide, owned, owned, resp, near, near),
        check_vma=False,
    )
```

```python
import math

import jax
import jax.numpy as jnp
from jax import lax
from jax.experimental import pallas as pl
from jax.experimental.pallas import tpu as pltpu
from jax.sharding import PartitionSpec as P

HD = 128
SBLK = 32
MESH = pl.DeviceIdType.MESH
NEG = -1e30
F32 = jnp.float32
BF = jnp.bfloat16
LOG2E = 1.4426950408889634

NX, NY, NZ, NZH = 4, 8, 8, 4
RESP = 256
PROWS = 64
RL = 2 * RESP
LANES = RL + 2 * PROWS
GROUP = 512
HALF = 64


def dot_t(a, b):
    return lax.dot_general(a, b, (((1,), (1,)), ((), ())), preferred_element_type=F32)


def dot_n(a, b):
    return lax.dot_general(a, b, (((1,), (0,)), ((), ())), preferred_element_type=F32)


def dot_l(a, b):
    return lax.dot_general(a, b, (((0,), (0,)), ((), ())), preferred_element_type=F32)


def kernel(
    pq, pg, po, kc, vc, ks, vs, rq, rg, ro, rk, rv, ln,
    o_dq, o_dk, o_dv, o_rdq, o_rdk, o_rdv,
    qm, gm, om, codes, deq, table, rsend, rtab, kr, vr, S, Sr, dqs, dqt,
    gout, r1, ady, adz, ray, raz, bdy, bdz, rby, rbz, fin, rfin, rgs, rgr,
    in_sem, rin_sem, out_sem,
    p_ss, p_rs, q_ss, q_rs, h_ss, h_rs, d_ss, d_rs, e_ss, e_rs, ya_ss, ya_rs, za_ss, za_rs,
    yb_ss, yb_rs, zb_ss, zb_rs, f_ss, f_rs, g_ss, g_rs,
):
    p = lax.axis_index("prompt")
    s = lax.axis_index("sample")
    x, zh = p // 4, p % 4
    y, zl, c = s // 4, (s // 2) % 2, s % 2
    z = zh * 2 + zl
    sg = 2 * zl - 1
    hy = y % 2
    inv = 1.0 / math.sqrt(HD)

    def dev(xx, yy, zz, cc):
        return (xx * 4 + zz // 2, yy * 4 + (zz % 2) * 2 + cc)

    def wrap(v, n):
        return lax.rem(v + 2 * n, n)

    def remote(src, dst, ss, rs, to):
        return pltpu.make_async_remote_copy(src, dst, ss, rs, device_id=to, device_id_type=MESH)

    sib = dev(x, y, z, 1 - c)

    bar = pltpu.get_barrier_semaphore()
    partners = []
    for dx in range(NX):
        for dz in range(NZ):
            if dx or dz:
                partners.append(dev(wrap(x + dx, NX), y, wrap(z + dz, NZ), c))
    for dy in range(1, NY):
        partners.append(dev(x, wrap(y + dy, NY), z, c))
    for dx in range(NX):
        for zz in range(2):
            partners.append(dev(wrap(x + dx, NX), y, zh * 2 + zz, 1 - c))
    for to in partners:
        pl.semaphore_signal(bar, inc=1, device_id=to, device_id_type=MESH)

    @pl.when(c == 0)
    def _():
        pltpu.make_async_copy(kc, codes, in_sem.at[12]).start()

    @pl.when(c == 1)
    def _():
        pltpu.make_async_copy(vc, codes, in_sem.at[12]).start()

    rloads = []
    for g in range(NX):
        for i, ref in enumerate((rk, rv)):
            rloads.append(
                pltpu.make_async_copy(
                    ref.at[0, :, pl.ds(g * HD, HD)], rsend.at[g, pl.ds(16 * i, 16)], rin_sem.at[g * 2 + i]
                )
            )
    for cp in rloads:
        cp.start()
    loads = []
    for i, (pref, rref, dst) in enumerate(((pq, rq, qm), (pg, rg, gm), (po, ro, om))):
        for h in range(2):
            loads.append(
                pltpu.make_async_copy(
                    rref.at[0, :, pl.ds(h * HD, HD)], dst.at[pl.ds(h * RESP, RESP)], in_sem.at[i * 4 + h]
                )
            )
            loads.append(
                pltpu.make_async_copy(
                    pref.at[:, pl.ds(h * HD, HD)], dst.at[pl.ds(RL + h * PROWS, PROWS)], in_sem.at[i * 4 + 2 + h]
                )
            )
    for cp in loads:
        cp.start()

    pltpu.make_async_copy(kc, codes, in_sem.at[12]).wait()
    for g in range(NX):
        for b in range(128 // SBLK):
            scale = jnp.where(c == 0, ks[b, g], vs[b, g])
            block = codes[b * SBLK : (b + 1) * SBLK, g * HD : (g + 1) * HD].astype(F32) * scale
            deq[g, b * SBLK : (b + 1) * SBLK, :] = block.astype(BF)
    own_rows = pl.ds(pl.multiple_of(x * HALF, HALF), HALF)
    for half in range(2):
        table[c, zh, half, own_rows, :] = deq[x, half * HALF : (half + 1) * HALF, :]
    for cp in rloads:
        cp.wait()

    pl.semaphore_wait(bar, len(partners))

    pcopies = []

    def psend(xt, zt, half):
        src = deq.at[xt, pl.ds(pl.multiple_of(half * HALF, HALF), HALF)]
        cp = remote(
            src, table.at[c, zh, half, own_rows], p_ss.at[len(pcopies)], p_rs.at[half, p], dev(xt, y, zt, c)
        )
        cp.start()
        pcopies.append(cp)

    for d in (3, 2, 1):
        for dx in (2, 1, 3, 0):
            psend(wrap(x + dx, NX), wrap(z + sg * d, NZ), hy)
    for dx in (2, 1, 3):
        for half in range(2):
            psend(wrap(x + dx, NX), z, half)
    qcopies = []
    for k in range(1, 16):
        pt = wrap(p + k, 16)
        cp = remote(rsend.at[pt // 4], rtab.at[p], q_ss.at[k], q_rs.at[p], (pt, s))
        cp.start()
        qcopies.append(cp)
    rtab[p] = rsend[x]

    groups = [zh, wrap(zh + sg, NZH), wrap(zh - sg, NZH), wrap(zh + 2, NZH)]

    dcopies, hcopies = [], []

    def hand(k, half, part, sem):
        cp = remote(part, part, d_ss.at[k, half], d_rs.at[groups[k], sem], sib)
        cp.start()
        dcopies.append(cp)

    for dx in (1, 3, 2):
        xs = wrap(x + dx, NX)
        rows = pl.ds(pl.multiple_of(xs * HALF, HALF), HALF)
        for half in range(2):
            piece = table.at[c, zh, half, rows]
            remote(piece, piece, p_ss.at[0], p_rs.at[half, xs * 4 + zh], sib).wait_recv()
    hand(0, 0, table.at[c, zh], 0)
    for k in range(1, 4):
        zg = groups[k]
        for i in range(2):
            for xs in (2 * i, 2 * i + 1):
                piece = table.at[c, zg, hy, pl.ds(xs * HALF, HALF)]
                remote(piece, piece, p_ss.at[0], p_rs.at[hy, xs * 4 + zg], sib).wait_recv()
            part = table.at[c, zg, hy, pl.ds(i * 2 * HALF, 2 * HALF)]
            cp = remote(part, part, h_ss.at[k - 1, i], h_rs.at[zg, i], dev(x, wrap(y + 1 - 2 * i, NY), z, c))
            cp.start()
            hcopies.append(cp)
        hand(k, 0, table.at[c, zg, hy], hy)

    for cp in loads:
        cp.wait()
    length = ln[0]
    live = lax.broadcasted_iota(jnp.int32, (RESP, HD), 0) < length
    for h in range(2):
        block = gm[h * RESP : (h + 1) * RESP, :]
        gm[h * RESP : (h + 1) * RESP, :] = jnp.where(live, block, jnp.zeros_like(block))
    delta = jnp.sum((gm[...].astype(F32) * om[...].astype(F32)).T, axis=0, keepdims=True)

    for k in range(1, 4):
        zg = groups[k]
        for i in range(2):
            part = table.at[c, zg, 1 - hy, pl.ds(i * 2 * HALF, 2 * HALF)]
            remote(part, part, h_ss.at[0, 0], h_rs.at[zg, i], sib).wait_recv()
        hand(k, 1, table.at[c, zg, 1 - hy], 1 - hy)

    for k in range(1, 16):
        ps = wrap(p + k, 16)
        remote(rtab.at[ps], rtab.at[ps], q_ss.at[0], q_rs.at[ps], sib).wait_recv()
    for i in range(16):
        kr[i * 16 : (i + 1) * 16, :] = rtab[i, 0:16, :]
        vr[i * 16 : (i + 1) * 16, :] = rtab[i, 16:32, :]

    other = table.at[1 - c, zh]
    remote(other, other, d_ss.at[0, 0], d_rs.at[zh, 0], sib).wait_recv()
    for k in range(1, 4):
        for half in range(2):
            other = table.at[1 - c, groups[k], half]
            remote(other, other, d_ss.at[0, 0], d_rs.at[groups[k], half], sib).wait_recv()

    u = lax.broadcasted_iota(jnp.int32, (RESP, RESP), 0)
    t = lax.broadcasted_iota(jnp.int32, (RESP, RESP), 1)
    near = (u <= t) & (u < length)
    sr = dot_t(kr[...], qm[0:RL, :])
    tops = []
    for h in range(2):
        part = jnp.where(near, sr[:, h * RESP : (h + 1) * RESP], NEG)
        Sr[:, h * RESP : (h + 1) * RESP] = part
        tops.append(jnp.max(part, axis=0, keepdims=True))
    top = jnp.concatenate(tops + [jnp.full((1, 2 * PROWS), NEG, F32)], axis=1)

    def group_of(k):
        step = jnp.where(k == 1, sg, jnp.where(k == 2, -sg, jnp.where(k == 3, 2, 0)))
        return lax.rem(zh + step + 4, 4)

    def scores(k, top):
        zg = group_of(k)
        keys = table[0, zg].reshape(GROUP, HD)
        far = dot_t(keys, qm[0:RL, :])
        S[zg, :, 0:RL] = far
        row = lax.broadcasted_iota(jnp.int32, (GROUP, 2 * PROWS), 0)
        lane = lax.broadcasted_iota(jnp.int32, (GROUP, 2 * PROWS), 1)
        place = ((row // HALF) % NX) * GROUP + zg * 128 + (row // 256) * HALF + row % HALF
        own = dot_t(keys, qm[RL:LANES, :])
        own = jnp.where(place <= s * PROWS + lane % PROWS, own, NEG)
        S[zg, :, RL:LANES] = own
        best = jnp.concatenate([jnp.max(far, axis=0, keepdims=True), jnp.max(own, axis=0, keepdims=True)], axis=1)
        return jnp.maximum(top, best)

    top = lax.fori_loop(0, 4, scores, top)

    er = jnp.exp2((Sr[...] - top[:, 0:RL]) * (inv * LOG2E))
    Sr[...] = er
    total = jnp.concatenate([jnp.sum(er, axis=0, keepdims=True), jnp.zeros((1, 2 * PROWS), F32)], axis=1)

    def powers(k, total):
        zg = group_of(k)
        e = jnp.exp2((S[zg] - top) * (inv * LOG2E))
        S[zg] = e
        return total + jnp.sum(e, axis=0, keepdims=True)

    total = lax.fori_loop(0, 4, powers, total)
    rtotal = 1.0 / total

    prob = Sr[...] * rtotal[:, 0:RL]
    dp = dot_t(vr[...], gm[0:RL, :])
    ds = (prob * (dp - delta[:, 0:RL])).astype(BF)
    dqt[:, 0:RL] = dot_l(kr[...], ds)
    dqt[:, RL:LANES] = jnp.zeros((HD, 2 * PROWS), F32)
    dkr = (dot_n(ds, qm[0:RL, :]) * inv).astype(BF)
    dvr = dot_n(prob.astype(BF), gm[0:RL, :]).astype(BF)
    for i in range(16):
        rgs[i, 0:16, :] = dkr[i * 16 : (i + 1) * 16, :]
        rgs[i, 16:32, :] = dvr[i * 16 : (i + 1) * 16, :]
    gcopies = []
    for k in range(1, 16):
        pt = wrap(p + k, 16)
        cp = remote(rgs.at[pt], rgr.at[p], g_ss.at[k], g_rs.at[p], (pt, s))
        cp.start()
        gcopies.append(cp)
    rgr[p] = rgs[p]

    def pair(zg, kv, i):
        rows = pl.ds(pl.multiple_of((2 * i + 1 - c) * 128, 128), 128)
        got = r1.at[kv, zg, pl.ds(i * 128, 128)]
        return remote(gout.at[kv, zg, rows], got, e_ss.at[zg, kv * 2 + i], e_rs.at[zg, kv * 2 + i], sib)

    def ysend(zg, d):
        yt = wrap(y + d, NY)
        rows = pl.ds(pl.multiple_of(zg * 32, 32), 32)
        return remote(ady.at[yt, rows], ray.at[d, rows], ya_ss.at[zg, d], ya_rs.at[zg, d], dev(x, yt, z, c))

    def zsend(zt):
        return remote(adz.at[zt], raz.at[z], za_ss.at[zt], za_rs.at[z], dev(x, y, zt, c))

    def spread(k):
        zg = group_of(k)
        for kv in range(2):
            for i in range(2):
                pair(zg, kv, i).wait_recv()
        for i in range(2):
            zt = zg * 2 + i
            keep = pl.ds(pl.multiple_of((2 * i + c) * 128, 128), 128)
            got = pl.ds(i * 128, 128)
            both = gout[0, zg, keep, :].astype(F32) + r1[0, zg, got, :].astype(F32)
            both = both.astype(BF)
            rows = pl.ds(pl.multiple_of(zt * 16, 16), 16)
            for yy in range(NY):
                ady[yy, rows, :] = both[yy * 16 : (yy + 1) * 16, :]
            both = gout[1, zg, keep, :].astype(F32) + r1[1, zg, got, :].astype(F32)
            adz[zt] = both.astype(BF)
        for d in (4, 3, 5, 2, 6, 1, 7):
            ysend(zg, d).start()
        for i in range(2):
            zt = zg * 2 + i

            @pl.when(zt != z)
            def _():
                zsend(zt).start()

    def grads(k, _):
        zg = group_of(k)
        prob = S[zg] * rtotal
        dp = dot_t(table[1, zg].reshape(GROUP, HD), gm[...])
        ds = (prob * (dp - delta)).astype(BF)
        dqt[...] += dot_l(table[0, zg].reshape(GROUP, HD), ds)
        for kv in range(2):
            if kv == 0:
                sums = (dot_n(ds, qm[...]) * inv).astype(BF)
            else:
                sums = dot_n(prob.astype(BF), gm[...]).astype(BF)
            for half in range(2):
                for xs in range(NX):
                    start = half * 256 + xs * HALF
                    to = xs * 128 + half * HALF
                    gout[kv, zg, to : to + HALF, :] = sums[start : start + HALF, :]
        for kv in range(2):
            for i in range(2):
                pair(zg, kv, i).start()

        @pl.when(k > 0)
        def _():
            spread(k - 1)

        return 0

    lax.fori_loop(0, 4, grads, 0)
    spread(3)

    dqs[...] = (dqt[...].T * inv).astype(BF)
    outs = []
    for h in range(2):
        outs.append(
            pltpu.make_async_copy(
                dqs.at[pl.ds(h * RESP, RESP)], o_rdq.at[0, :, pl.ds(h * HD, HD)], out_sem.at[h]
            )
        )
        outs.append(
            pltpu.make_async_copy(
                dqs.at[pl.ds(RL + h * PROWS, PROWS)], o_dq.at[:, pl.ds(h * HD, HD)], out_sem.at[2 + h]
            )
        )
    for cp in outs:
        cp.start()

    for zg in range(4):
        for d in range(1, 8):
            ysend(zg, d).wait_recv()
    acc = ady[y].astype(F32)
    for d in range(1, 8):
        acc += ray[d].astype(F32)
    bdy[...] = acc.astype(BF)
    zb, yb = [], []
    for d in range(1, 8):
        zt = wrap(z + d, NZ)
        cp = remote(
            bdy.at[pl.ds(pl.multiple_of(zt * 16, 16), 16)], rbz.at[d], zb_ss.at[d], zb_rs.at[d], dev(x, y, zt, c)
        )
        cp.start()
        zb.append(cp)
    for d in range(1, 8):
        zs = wrap(z + d, NZ)
        remote(adz.at[zs], raz.at[zs], za_ss.at[0], za_rs.at[zs], sib).wait_recv()
    acc = adz[z].astype(F32)
    for d in range(1, 8):
        acc += raz[wrap(z + d, NZ)].astype(F32)
    bdz[...] = acc.astype(BF)
    for d in range(1, 8):
        yt = wrap(y + d, NY)
        cp = remote(
            bdz.at[pl.ds(pl.multiple_of(yt * 16, 16), 16)], rby.at[d], yb_ss.at[d], yb_rs.at[d], dev(x, yt, z, c)
        )
        cp.start()
        yb.append(cp)
    for cp in gcopies:
        cp.wait_send()
    for k in range(1, 16):
        ps = wrap(p + k, 16)
        remote(rgr.at[ps], rgr.at[ps], g_ss.at[0], g_rs.at[ps], sib).wait_recv()
    for g in range(NX):
        acc = rgr[g * 4].astype(F32)
        for i in range(1, 4):
            acc += rgr[g * 4 + i].astype(F32)
        acc = acc.astype(BF)
        o_rdk[0, :, g * HD : (g + 1) * HD] = acc[0:16, :]
        o_rdv[0, :, g * HD : (g + 1) * HD] = acc[16:32, :]

    for cp in zb:
        cp.wait_recv()
    acc = bdy[pl.ds(pl.multiple_of(z * 16, 16), 16), :].astype(F32)
    for d in range(1, 8):
        acc += rbz[d].astype(F32)
    fin[0:16, :] = acc.astype(BF)
    for cp in yb:
        cp.wait_recv()
    acc = bdz[pl.ds(pl.multiple_of(y * 16, 16), 16), :].astype(F32)
    for d in range(1, 8):
        acc += rby[d].astype(F32)
    fin[16:32, :] = acc.astype(BF)

    xo = 2 * zl + c
    zf, cf = x // 2, x % 2

    def final(i):
        zz, cc = i // 2, i % 2
        same = (xo == x) & (zl == zz) & (c == cc)
        return same, remote(fin, rfin.at[x], f_ss.at[i], f_rs.at[x], dev(xo, y, zh * 2 + zz, cc))

    for i in range(4):
        same, cp = final(i)

        @pl.when(jnp.logical_not(same))
        def _():
            cp.start()

        @pl.when(same)
        def _():
            rfin[x] = fin[...]

    for xs in range(NX):
        mine = (x == xs) & (zf == zl) & (cf == c)

        @pl.when(jnp.logical_not(mine))
        def _():
            remote(fin, rfin.at[xs], f_ss.at[0], f_rs.at[xs], sib).wait_recv()

    spot = zl * 2 + c
    for xs in range(NX):
        tile = rfin[xs].astype(F32)
        for half, out in ((0, o_dk), (16, o_dv)):
            rows = tile[half : half + 4, :]
            for i in range(1, 4):
                rows = jnp.where(spot == i, tile[half + 4 * i : half + 4 * i + 4, :], rows)
            out[:, xs * HD : (xs + 1) * HD] = rows.astype(BF)

    for i in range(4):
        same, cp = final(i)

        @pl.when(jnp.logical_not(same))
        def _():
            cp.wait_send()

    for cp in pcopies + qcopies + hcopies + dcopies + zb + yb:
        cp.wait_send()
    for zg in range(4):
        for kv in range(2):
            for i in range(2):
                pair(zg, kv, i).wait_send()
        for d in range(1, 8):
            ysend(zg, d).wait_send()
    for d in range(1, 8):
        zsend(wrap(z + d, NZ)).wait_send()
    for cp in outs:
        cp.wait()


def place(*refs):
    for i in range(6):
        refs[6 + i][...] = refs[i][...]


def shards(*args):
    hbm = pl.BlockSpec(memory_space=pl.ANY)
    smem = pl.BlockSpec(memory_space=pltpu.SMEM)
    vmem = pl.BlockSpec(memory_space=pltpu.VMEM)
    dma = pltpu.SemaphoreType.DMA
    shape = jax.ShapeDtypeStruct
    made = pl.pallas_call(
        kernel,
        out_shape=(
            shape((PROWS, 256), BF),
            shape((4, 512), BF),
            shape((4, 512), BF),
            shape((1, RESP, 256), BF),
            shape((1, 16, 512), BF),
            shape((1, 16, 512), BF),
        ),
        in_specs=[hbm] * 5 + [smem] * 2 + [hbm] * 5 + [smem],
        out_specs=(hbm, vmem, vmem, hbm, vmem, vmem),
        scratch_shapes=[
            pltpu.VMEM((LANES, HD), BF),
            pltpu.VMEM((LANES, HD), BF),
            pltpu.VMEM((LANES, HD), BF),
            pltpu.VMEM((128, 512), BF),
            pltpu.VMEM((4, 128, HD), BF),
            pltpu.VMEM((2, 4, 2, GROUP // 2, HD), BF),
            pltpu.VMEM((4, 32, HD), BF),
            pltpu.VMEM((16, 32, HD), BF),
            pltpu.VMEM((RESP, HD), BF),
            pltpu.VMEM((RESP, HD), BF),
            pltpu.VMEM((4, GROUP, LANES), F32),
            pltpu.VMEM((RESP, RL), F32),
            pltpu.VMEM((LANES, HD), BF),
            pltpu.VMEM((HD, LANES), F32),
            pltpu.VMEM((2, 4, GROUP, HD), BF),
            pltpu.VMEM((2, 4, 256, HD), BF),
            pltpu.VMEM((8, 128, HD), BF),
            pltpu.VMEM((8, 128, HD), BF),
            pltpu.VMEM((8, 128, HD), BF),
            pltpu.VMEM((8, 128, HD), BF),
            pltpu.VMEM((128, HD), BF),
            pltpu.VMEM((128, HD), BF),
            pltpu.VMEM((8, 16, HD), BF),
            pltpu.VMEM((8, 16, HD), BF),
            pltpu.VMEM((32, HD), BF),
            pltpu.VMEM((4, 32, HD), BF),
            pltpu.VMEM((16, 32, HD), BF),
            pltpu.VMEM((16, 32, HD), BF),
            dma((13,)),
            dma((8,)),
            dma((4,)),
            dma((18,)),
            dma((2, 16)),
            dma((16,)),
            dma((16,)),
            dma((3, 2)),
            dma((4, 2)),
            dma((4, 2)),
            dma((4, 2)),
            dma((4, 4)),
            dma((4, 4)),
            dma((4, 8)),
            dma((4, 8)),
        ]
        + [dma((8,))] * 6
        + [dma((4,)), dma((4,)), dma((16,)), dma((16,))],
        compiler_params=pltpu.CompilerParams(
            collective_id=0, has_side_effects=True, vmem_limit_bytes=60 * 1024 * 1024
        ),
        name="attention_backward",
    )(*args)
    return pl.pallas_call(
        place,
        out_shape=tuple(shape(a.shape, a.dtype) for a in made),
        in_specs=[vmem] * 6,
        out_specs=[vmem] * 6,
        compiler_params=pltpu.CompilerParams(vmem_limit_bytes=60 * 1024 * 1024),
        name="place_outputs",
    )(*made)


def solution(mesh):
    wide = P("sample", "prompt")
    block = P("prompt", None)
    resp = P("sample", None, "prompt")
    near = P("sample", "prompt", None)
    owned = P(("prompt", "sample"), None)
    return jax.shard_map(
        shards,
        mesh=mesh,
        in_specs=(wide, wide, wide, block, block, block, block, resp, resp, resp, near, near, P("sample")),
        out_specs=(wide, owned, owned, resp, near, near),
        check_vma=False,
    )
```

```python
import math

import jax
import jax.numpy as jnp
from jax import lax
from jax.experimental import pallas as pl
from jax.experimental.pallas import tpu as pltpu
from jax.sharding import PartitionSpec as P

HD = 128
SBLK = 32
MESH = pl.DeviceIdType.MESH
NEG = -1e30
F32 = jnp.float32
BF = jnp.bfloat16
LOG2E = 1.4426950408889634

NX, NY, NZ, NZH = 4, 8, 8, 4
RESP = 256
PROWS = 64
RL = 2 * RESP
LANES = RL + 2 * PROWS
GROUP = 512
HALF = 64


def dot_t(a, b):
    return lax.dot_general(a, b, (((1,), (1,)), ((), ())), preferred_element_type=F32)


def dot_n(a, b):
    return lax.dot_general(a, b, (((1,), (0,)), ((), ())), preferred_element_type=F32)


def dot_l(a, b):
    return lax.dot_general(a, b, (((0,), (0,)), ((), ())), preferred_element_type=F32)


def kernel(
    pq, pg, po, kc, vc, ks, vs, rq, rg, ro, rk, rv, ln,
    o_dq, o_dk, o_dv, o_rdq, o_rdk, o_rdv,
    qm, gm, om, codes, deq, table, rsend, rtab, kr, vr, S, Sr, dqs, dqt,
    mx, sm, gout, r1, ady, adz, ray, raz, bdy, bdz, rby, rbz, fin, rfin, rgs, rgr, scl, lens,
    in_sem,
    p_ss, p_rs, q_ss, q_rs, h_ss, h_rs, d_ss, d_rs, e_ss, e_rs, ya_ss, ya_rs, za_ss, za_rs,
    yb_ss, yb_rs, zb_ss, zb_rs, f_ss, f_rs, g_ss, g_rs,
):
    p = lax.axis_index("prompt")
    s = lax.axis_index("sample")
    x, zh = p // 4, p % 4
    y, zl, c = s // 4, (s // 2) % 2, s % 2
    z = zh * 2 + zl
    sg = 2 * zl - 1
    hy = y % 2
    inv = 1.0 / math.sqrt(HD)

    def dev(xx, yy, zz, cc):
        return (xx * 4 + zz // 2, yy * 4 + (zz % 2) * 2 + cc)

    def wrap(v, n):
        return lax.rem(v + 2 * n, n)

    def remote(src, dst, ss, rs, to):
        return pltpu.make_async_remote_copy(src, dst, ss, rs, device_id=to, device_id_type=MESH)

    sib = dev(x, y, z, 1 - c)

    bar = pltpu.get_barrier_semaphore()
    partners = []
    for dx in range(NX):
        for dz in range(NZ):
            if dx or dz:
                partners.append(dev(wrap(x + dx, NX), y, wrap(z + dz, NZ), c))
    for dy in range(1, NY):
        partners.append(dev(x, wrap(y + dy, NY), z, c))
    for dx in range(NX):
        for zz in range(2):
            partners.append(dev(wrap(x + dx, NX), y, zh * 2 + zz, 1 - c))
    for to in partners:
        pl.semaphore_signal(bar, inc=1, device_id=to, device_id_type=MESH)

    def share(codes_ref, scale_ref):
        pltpu.make_async_copy(codes_ref, codes, in_sem.at[0]).start()
        pltpu.make_async_copy(scale_ref, scl, in_sem.at[1]).start()

    @pl.when(c == 0)
    def _():
        share(kc, ks)

    @pl.when(c == 1)
    def _():
        share(vc, vs)

    pltpu.make_async_copy(ln, lens, in_sem.at[2]).start()
    rloads = []
    for g in range(NX):
        for i, ref in enumerate((rk, rv)):
            rloads.append(
                pltpu.make_async_copy(
                    ref.at[0, :, pl.ds(g * HD, HD)], rsend.at[g, pl.ds(16 * i, 16)], in_sem.at[3]
                )
            )
    for cp in rloads:
        cp.start()
    loads = []
    for i, (pref, rref, dst) in enumerate(((pq, rq, qm), (pg, rg, gm), (po, ro, om))):
        for h in range(2):
            loads.append(
                pltpu.make_async_copy(
                    rref.at[0, :, pl.ds(h * HD, HD)], dst.at[pl.ds(h * RESP, RESP)], in_sem.at[4 + i]
                )
            )
            loads.append(
                pltpu.make_async_copy(
                    pref.at[:, pl.ds(h * HD, HD)], dst.at[pl.ds(RL + h * PROWS, PROWS)], in_sem.at[4 + i]
                )
            )
    for cp in loads:
        cp.start()

    pltpu.make_async_copy(kc, codes, in_sem.at[0]).wait()
    pltpu.make_async_copy(ks, scl, in_sem.at[1]).wait()
    for g in range(NX):
        for b in range(128 // SBLK):
            block = codes[b * SBLK : (b + 1) * SBLK, g * HD : (g + 1) * HD].astype(F32) * scl[b, g]
            deq[g, b * SBLK : (b + 1) * SBLK, :] = block.astype(BF)
    own_rows = pl.ds(pl.multiple_of(x * HALF, HALF), HALF)
    for half in range(2):
        table[c, zh, half, own_rows, :] = deq[x, half * HALF : (half + 1) * HALF, :]
    pltpu.make_async_copy(rsend, rsend, in_sem.at[3]).wait()

    pl.semaphore_wait(bar, len(partners))

    def psend(xt, zt, half, sem):
        src = deq.at[xt, pl.ds(pl.multiple_of(half * HALF, HALF), HALF)]
        remote(src, table.at[c, zh, half, own_rows], p_ss.at[0], sem, dev(xt, y, zt, c)).start()

    for d in (1, 2, 3):
        for dx in (2, 1, 3, 0):
            psend(wrap(x + dx, NX), wrap(z + sg * d, NZ), hy, p_rs.at[zh, x // 2])
    for dx in (2, 1, 3):
        for half in range(2):
            psend(wrap(x + dx, NX), z, half, p_rs.at[4, 0])
    for k in range(1, 16):
        pt = wrap(p + k, 16)
        remote(rsend.at[pt // 4], rtab.at[p], q_ss.at[0], q_rs.at[0], (pt, s)).start()
    rtab[p] = rsend[x]

    groups = [zh, wrap(zh + sg, NZH), wrap(zh - sg, NZH), wrap(zh + 2, NZH)]

    for i, dst in enumerate((qm, gm, om)):
        pltpu.make_async_copy(dst, dst, in_sem.at[4 + i]).wait()
    pltpu.make_async_copy(ln, lens, in_sem.at[2]).wait()
    length = lens[0]
    live = lax.broadcasted_iota(jnp.int32, (RESP, HD), 0) < length
    for h in range(2):
        block = gm[h * RESP : (h + 1) * RESP, :]
        gm[h * RESP : (h + 1) * RESP, :] = jnp.where(live, block, jnp.zeros_like(block))
    delta = jnp.sum((gm[...].astype(F32) * om[...].astype(F32)).T, axis=0, keepdims=True)

    def hand(k, part):
        remote(part, part, d_ss.at[0], d_rs.at[groups[k]], sib).start()

    def take_near():
        part = deq.at[pl.ds(0, 3)]
        remote(part, part, p_ss.at[0], p_rs.at[4, 0], sib).wait_recv()
        hand(0, table.at[c, zh])

    def take_far(k):
        zg = groups[k]
        for i in range(2):
            part = table.at[c, zg, hy, pl.ds(i * 2 * HALF, 2 * HALF)]
            remote(part, part, p_ss.at[0], p_rs.at[zg, i], sib).wait_recv()
            remote(part, part, h_ss.at[0], h_rs.at[zg, i], dev(x, wrap(y + 1 - 2 * i, NY), z, c)).start()
        hand(k, table.at[c, zg, hy])

    def take_beside(k):
        zg = groups[k]
        for i in range(2):
            part = table.at[c, zg, 1 - hy, pl.ds(i * 2 * HALF, 2 * HALF)]
            remote(part, part, h_ss.at[0], h_rs.at[zg, i], sib).wait_recv()
        hand(k, table.at[c, zg, 1 - hy])

    def group_of(k):
        step = jnp.where(k == 1, sg, jnp.where(k == 2, -sg, jnp.where(k == 3, 2, 0)))
        return lax.rem(zh + step + 4, 4)

    def absorb(k):
        zg = group_of(k)
        other = table.at[1 - c, zg]
        remote(other, other, d_ss.at[0], d_rs.at[zg], sib).wait_recv()
        keys = table[0, zg].reshape(GROUP, HD)
        far = dot_t(keys, qm[0:RL, :])
        best = jnp.max(far, axis=0, keepdims=True)
        mx[zg, :, 0:RL] = best
        far = jnp.exp2((far - best) * (inv * LOG2E))
        sm[zg, :, 0:RL] = jnp.sum(far, axis=0, keepdims=True)
        S[zg, :, 0:RL] = far
        row = lax.broadcasted_iota(jnp.int32, (GROUP, 2 * PROWS), 0)
        lane = lax.broadcasted_iota(jnp.int32, (GROUP, 2 * PROWS), 1)
        place = ((row // HALF) % NX) * GROUP + zg * 128 + (row // 256) * HALF + row % HALF
        own = dot_t(keys, qm[RL:LANES, :])
        own = jnp.where(place <= s * PROWS + lane % PROWS, own, NEG)
        best = jnp.max(own, axis=0, keepdims=True)
        mx[zg, :, RL:LANES] = best
        own = jnp.exp2((own - best) * (inv * LOG2E))
        sm[zg, :, RL:LANES] = jnp.sum(own, axis=0, keepdims=True)
        S[zg, :, RL:LANES] = own

    take_near()
    take_far(1)
    absorb(0)
    take_far(2)
    take_far(3)
    take_beside(1)
    take_beside(2)
    take_beside(3)

    def absorb_loop(k, _):
        absorb(k)
        return 0

    lax.fori_loop(1, 4, absorb_loop, 0)

    part = rtab.at[pl.ds(0, 15)]
    remote(part, part, q_ss.at[0], q_rs.at[0], sib).wait_recv()
    for i in range(16):
        kr[i * 16 : (i + 1) * 16, :] = rtab[i, 0:16, :]
        vr[i * 16 : (i + 1) * 16, :] = rtab[i, 16:32, :]
    u = lax.broadcasted_iota(jnp.int32, (RESP, RESP), 0)
    t = lax.broadcasted_iota(jnp.int32, (RESP, RESP), 1)
    near = (u <= t) & (u < length)
    sr = dot_t(kr[...], qm[0:RL, :])
    tops, sums = [], []
    for h in range(2):
        part = jnp.where(near, sr[:, h * RESP : (h + 1) * RESP], NEG)
        best = jnp.max(part, axis=0, keepdims=True)
        part = jnp.exp2((part - best) * (inv * LOG2E))
        Sr[:, h * RESP : (h + 1) * RESP] = part
        tops.append(best)
        sums.append(jnp.sum(part, axis=0, keepdims=True))
    tops = jnp.concatenate(tops + [jnp.full((1, 2 * PROWS), NEG, F32)], axis=1)
    sums = jnp.concatenate(sums + [jnp.zeros((1, 2 * PROWS), F32)], axis=1)

    top = tops
    for zg in range(4):
        top = jnp.maximum(top, mx[zg])
    rscale = jnp.exp2((tops - top) * (inv * LOG2E))
    total = sums * rscale
    scales = []
    for zg in range(4):
        scale = jnp.exp2((mx[zg] - top) * (inv * LOG2E))
        total += sm[zg] * scale
        scales.append(scale)
    rtotal = 1.0 / total
    rscale = rscale * rtotal
    for zg in range(4):
        mx[zg] = scales[zg] * rtotal

    def pair(zg, kv, i):
        rows = pl.ds(pl.multiple_of((2 * i + 1 - c) * 128, 128), 128)
        got = r1.at[kv, zg, pl.ds(i * 128, 128)]
        return remote(gout.at[kv, zg, rows], got, e_ss.at[0], e_rs.at[zg], sib)

    def ysend(zg, d):
        yt = wrap(y + d, NY)
        rows = pl.ds(pl.multiple_of(zg * 32, 32), 32)
        return remote(ady.at[yt, rows], ray.at[d, rows], ya_ss.at[0], ya_rs.at[0], dev(x, yt, z, c))

    def zsend(zt):
        return remote(adz.at[zt], raz.at[z], za_ss.at[0], za_rs.at[0], dev(x, y, zt, c))

    def spread(k):
        zg = group_of(k)
        part = gout.at[0, zg]
        remote(part, part, e_ss.at[0], e_rs.at[zg], sib).wait_recv()
        for i in range(2):
            zt = zg * 2 + i
            keep = pl.ds(pl.multiple_of((2 * i + c) * 128, 128), 128)
            got = pl.ds(i * 128, 128)
            both = gout[0, zg, keep, :].astype(F32) + r1[0, zg, got, :].astype(F32)
            both = both.astype(BF)
            rows = pl.ds(pl.multiple_of(zt * 16, 16), 16)
            for yy in range(NY):
                ady[yy, rows, :] = both[yy * 16 : (yy + 1) * 16, :]
            both = gout[1, zg, keep, :].astype(F32) + r1[1, zg, got, :].astype(F32)
            adz[zt] = both.astype(BF)
        for d in (4, 3, 5, 2, 6, 1, 7):
            ysend(zg, d).start()
        for i in range(2):
            zt = zg * 2 + i

            @pl.when(zt != z)
            def _():
                zsend(zt).start()

    def grads(k, _):
        zg = group_of(k)
        prob = S[zg] * mx[zg]
        dp = dot_t(table[1, zg].reshape(GROUP, HD), gm[...])
        ds = (prob * (dp - delta)).astype(BF)
        dqt[...] += dot_l(table[0, zg].reshape(GROUP, HD), ds)
        for kv in range(2):
            if kv == 0:
                sums = (dot_n(ds, qm[...]) * inv).astype(BF)
            else:
                sums = dot_n(prob.astype(BF), gm[...]).astype(BF)
            for half in range(2):
                for xs in range(NX):
                    start = half * 256 + xs * HALF
                    to = xs * 128 + half * HALF
                    gout[kv, zg, to : to + HALF, :] = sums[start : start + HALF, :]
        for kv in range(2):
            for i in range(2):
                pair(zg, kv, i).start()

        @pl.when(k > 0)
        def _():
            spread(k - 1)

        return 0

    dqt[...] = jnp.zeros_like(dqt)
    lax.fori_loop(0, 4, grads, 0)

    prob = Sr[...] * rscale[:, 0:RL]
    dp = dot_t(vr[...], gm[0:RL, :])
    ds = (prob * (dp - delta[:, 0:RL])).astype(BF)
    dqt[:, 0:RL] += dot_l(kr[...], ds)
    dkr = (dot_n(ds, qm[0:RL, :]) * inv).astype(BF)
    dvr = dot_n(prob.astype(BF), gm[0:RL, :]).astype(BF)
    for i in range(16):
        rgs[i, 0:16, :] = dkr[i * 16 : (i + 1) * 16, :]
        rgs[i, 16:32, :] = dvr[i * 16 : (i + 1) * 16, :]
    spread(3)
    for k in range(1, 16):
        pt = wrap(p + k, 16)
        remote(rgs.at[pt], rgr.at[p], g_ss.at[0], g_rs.at[0], (pt, s)).start()
    rgr[p] = rgs[p]

    dqs[...] = (dqt[...].T * inv).astype(BF)
    outs = []
    for h in range(2):
        outs.append(
            pltpu.make_async_copy(
                dqs.at[pl.ds(h * RESP, RESP)], o_rdq.at[0, :, pl.ds(h * HD, HD)], in_sem.at[7]
            )
        )
        outs.append(
            pltpu.make_async_copy(
                dqs.at[pl.ds(RL + h * PROWS, PROWS)], o_dq.at[:, pl.ds(h * HD, HD)], in_sem.at[7]
            )
        )
    for cp in outs:
        cp.start()

    seven = ray.at[pl.ds(1, 7)]
    remote(seven, seven, ya_ss.at[0], ya_rs.at[0], sib).wait_recv()
    acc = ady[y].astype(F32)
    for d in range(1, 8):
        acc += ray[d].astype(F32)
    bdy[...] = acc.astype(BF)
    for d in range(1, 8):
        zt = wrap(z + d, NZ)
        cp = remote(
            bdy.at[pl.ds(pl.multiple_of(zt * 16, 16), 16)], rbz.at[d], zb_ss.at[0], zb_rs.at[0], dev(x, y, zt, c)
        )
        cp.start()
    remote(seven, seven, za_ss.at[0], za_rs.at[0], sib).wait_recv()
    acc = adz[z].astype(F32)
    for d in range(1, 8):
        acc += raz[wrap(z + d, NZ)].astype(F32)
    bdz[...] = acc.astype(BF)
    for d in range(1, 8):
        yt = wrap(y + d, NY)
        cp = remote(
            bdz.at[pl.ds(pl.multiple_of(yt * 16, 16), 16)], rby.at[d], yb_ss.at[0], yb_rs.at[0], dev(x, yt, z, c)
        )
        cp.start()
    part = rgr.at[pl.ds(0, 15)]
    remote(part, part, g_ss.at[0], g_rs.at[0], sib).wait_recv()
    for g in range(NX):
        acc = rgr[g * 4].astype(F32)
        for i in range(1, 4):
            acc += rgr[g * 4 + i].astype(F32)
        acc = acc.astype(BF)
        o_rdk[0, :, g * HD : (g + 1) * HD] = acc[0:16, :]
        o_rdv[0, :, g * HD : (g + 1) * HD] = acc[16:32, :]

    some = rbz.at[pl.ds(1, 7)]
    remote(some, some, zb_ss.at[0], zb_rs.at[0], sib).wait_recv()
    acc = bdy[pl.ds(pl.multiple_of(z * 16, 16), 16), :].astype(F32)
    for d in range(1, 8):
        acc += rbz[d].astype(F32)
    fin[0:16, :] = acc.astype(BF)
    remote(some, some, yb_ss.at[0], yb_rs.at[0], sib).wait_recv()
    acc = bdz[pl.ds(pl.multiple_of(y * 16, 16), 16), :].astype(F32)
    for d in range(1, 8):
        acc += rby[d].astype(F32)
    fin[16:32, :] = acc.astype(BF)

    xo = 2 * zl + c
    zf, cf = x // 2, x % 2

    def final(i):
        zz, cc = i // 2, i % 2
        same = (xo == x) & (zl == zz) & (c == cc)
        return same, remote(fin, rfin.at[x], f_ss.at[i], f_rs.at[x], dev(xo, y, zh * 2 + zz, cc))

    for i in range(4):
        same, cp = final(i)

        @pl.when(jnp.logical_not(same))
        def _():
            cp.start()

        @pl.when(same)
        def _():
            rfin[x] = fin[...]

    for xs in range(NX):
        mine = (x == xs) & (zf == zl) & (cf == c)

        @pl.when(jnp.logical_not(mine))
        def _():
            remote(fin, rfin.at[xs], f_ss.at[0], f_rs.at[xs], sib).wait_recv()

    spot = zl * 2 + c
    for xs in range(NX):
        tile = rfin[xs].astype(F32)
        for half, out in ((0, o_dk), (16, o_dv)):
            rows = tile[half : half + 4, :]
            for i in range(1, 4):
                rows = jnp.where(spot == i, tile[half + 4 * i : half + 4 * i + 4, :], rows)
            out[:, xs * HD : (xs + 1) * HD] = rows.astype(BF)

    for i in range(4):
        same, cp = final(i)

        @pl.when(jnp.logical_not(same))
        def _():
            cp.wait_send()

    def sent(part, sem):
        remote(part, part, sem.at[0], p_rs.at[0, 0], sib).wait_send()

    sent(gout.at[0, pl.ds(0, 3), pl.ds(0, 384)], p_ss)
    sent(rtab.at[pl.ds(0, 15)], q_ss)
    sent(gout.at[0, pl.ds(0, 2), pl.ds(0, 384)], h_ss)
    sent(table.at[0], d_ss)
    sent(gout.at[0], e_ss)
    sent(seven, ya_ss)
    sent(seven, za_ss)
    sent(some, yb_ss)
    sent(some, zb_ss)
    sent(rtab.at[pl.ds(0, 15)], g_ss)
    pltpu.make_async_copy(dqs, dqs, in_sem.at[7]).wait()


def place(*refs):
    for i in range(6):
        refs[6 + i][...] = refs[i][...]


def shards(*args):
    hbm = pl.BlockSpec(memory_space=pl.ANY)
    vmem = pl.BlockSpec(memory_space=pltpu.VMEM)
    dma = pltpu.SemaphoreType.DMA
    shape = jax.ShapeDtypeStruct
    made = pl.pallas_call(
        kernel,
        out_shape=(
            shape((PROWS, 256), BF),
            shape((4, 512), BF),
            shape((4, 512), BF),
            shape((1, RESP, 256), BF),
            shape((1, 16, 512), BF),
            shape((1, 16, 512), BF),
        ),
        in_specs=[hbm] * 13,
        out_specs=(hbm, vmem, vmem, hbm, vmem, vmem),
        scratch_shapes=[
            pltpu.VMEM((LANES, HD), BF),
            pltpu.VMEM((LANES, HD), BF),
            pltpu.VMEM((LANES, HD), BF),
            pltpu.VMEM((128, 512), BF),
            pltpu.VMEM((4, 128, HD), BF),
            pltpu.VMEM((2, 4, 2, GROUP // 2, HD), BF),
            pltpu.VMEM((4, 32, HD), BF),
            pltpu.VMEM((16, 32, HD), BF),
            pltpu.VMEM((RESP, HD), BF),
            pltpu.VMEM((RESP, HD), BF),
            pltpu.VMEM((4, GROUP, LANES), F32),
            pltpu.VMEM((RESP, RL), F32),
            pltpu.VMEM((LANES, HD), BF),
            pltpu.VMEM((HD, LANES), F32),
            pltpu.VMEM((4, 1, LANES), F32),
            pltpu.VMEM((4, 1, LANES), F32),
            pltpu.VMEM((2, 4, GROUP, HD), BF),
            pltpu.VMEM((2, 4, 256, HD), BF),
            pltpu.VMEM((8, 128, HD), BF),
            pltpu.VMEM((8, 128, HD), BF),
            pltpu.VMEM((8, 128, HD), BF),
            pltpu.VMEM((8, 128, HD), BF),
            pltpu.VMEM((128, HD), BF),
            pltpu.VMEM((128, HD), BF),
            pltpu.VMEM((8, 16, HD), BF),
            pltpu.VMEM((8, 16, HD), BF),
            pltpu.VMEM((32, HD), BF),
            pltpu.VMEM((4, 32, HD), BF),
            pltpu.VMEM((16, 32, HD), BF),
            pltpu.VMEM((16, 32, HD), BF),
            pltpu.SMEM((4, 4), F32),
            pltpu.SMEM((1,), jnp.int32),
            dma((8,)),
            dma((1,)),
            dma((5, 2)),
            dma((1,)),
            dma((1,)),
            dma((1,)),
            dma((4, 2)),
            dma((1,)),
            dma((4,)),
            dma((1,)),
            dma((4,)),
        ]
        + [dma((1,))] * 8
        + [dma((4,)), dma((4,)), dma((1,)), dma((1,))],
        compiler_params=pltpu.CompilerParams(
            collective_id=0, has_side_effects=True, vmem_limit_bytes=60 * 1024 * 1024
        ),
        name="attention_backward",
    )(*args)
    return pl.pallas_call(
        place,
        out_shape=tuple(shape(a.shape, a.dtype) for a in made),
        in_specs=[vmem] * 6,
        out_specs=[vmem] * 6,
        compiler_params=pltpu.CompilerParams(vmem_limit_bytes=60 * 1024 * 1024),
        name="place_outputs",
    )(*made)


def solution(mesh):
    wide = P("sample", "prompt")
    block = P("prompt", None)
    resp = P("sample", None, "prompt")
    near = P("sample", "prompt", None)
    owned = P(("prompt", "sample"), None)
    return jax.shard_map(
        shards,
        mesh=mesh,
        in_specs=(wide, wide, wide, block, block, block, block, resp, resp, resp, near, near, P("sample")),
        out_specs=(wide, owned, owned, resp, near, near),
        check_vma=False,
    )
```

```python
import math

import jax
import jax.numpy as jnp
from jax import lax
from jax.experimental import pallas as pl
from jax.experimental.pallas import tpu as pltpu
from jax.sharding import PartitionSpec as P

HD = 128
SBLK = 32
MESH = pl.DeviceIdType.MESH
NEG = -1e30
F32 = jnp.float32
BF = jnp.bfloat16
LOG2E = 1.4426950408889634

NX, NY, NZ, NZH = 4, 8, 8, 4
RESP = 256
PROWS = 64
RL = 2 * RESP
LANES = RL + 2 * PROWS
GROUP = 512
HALF = 64


def dot_t(a, b):
    return lax.dot_general(a, b, (((1,), (1,)), ((), ())), preferred_element_type=F32)


def dot_n(a, b):
    return lax.dot_general(a, b, (((1,), (0,)), ((), ())), preferred_element_type=F32)


def dot_l(a, b):
    return lax.dot_general(a, b, (((0,), (0,)), ((), ())), preferred_element_type=F32)


def kernel(
    pq, pg, po, kc, vc, ks, vs, rq, rg, ro, rk, rv, ln,
    o_dq, o_dk, o_dv, o_rdq, o_rdk, o_rdv,
    qm, gm, om, codes, deq, table, rsend, rtab, kr, vr, S, DP, Sr, dqs, dqt,
    mx, sm, gout, r1, ady, adz, ray, raz, bdy, bdz, rby, rbz, fin, rfin, rgs, rgr, scl, lens,
    in_sem,
    p_ss, p_rs, q_ss, q_rs, h_ss, h_rs, d_ss, d_rs, e_ss, e_rs, ya_ss, ya_rs, za_ss, za_rs,
    yb_ss, yb_rs, zb_ss, zb_rs, f_ss, f_rs, g_ss, g_rs,
):
    p = lax.axis_index("prompt")
    s = lax.axis_index("sample")
    x, zh = p // 4, p % 4
    y, zl, c = s // 4, (s // 2) % 2, s % 2
    z = zh * 2 + zl
    sg = 2 * zl - 1
    hy = y % 2
    inv = 1.0 / math.sqrt(HD)

    def dev(xx, yy, zz, cc):
        return (xx * 4 + zz // 2, yy * 4 + (zz % 2) * 2 + cc)

    def wrap(v, n):
        return lax.rem(v + 2 * n, n)

    def remote(src, dst, ss, rs, to):
        return pltpu.make_async_remote_copy(src, dst, ss, rs, device_id=to, device_id_type=MESH)

    sib = dev(x, y, z, 1 - c)

    bar = pltpu.get_barrier_semaphore()
    partners = []
    for dx in range(NX):
        for dz in range(NZ):
            if dx or dz:
                partners.append(dev(wrap(x + dx, NX), y, wrap(z + dz, NZ), c))
    for dy in range(1, NY):
        partners.append(dev(x, wrap(y + dy, NY), z, c))
    for dx in range(NX):
        for zz in range(2):
            partners.append(dev(wrap(x + dx, NX), y, zh * 2 + zz, 1 - c))
    for to in partners:
        pl.semaphore_signal(bar, inc=1, device_id=to, device_id_type=MESH)

    def share(codes_ref, scale_ref):
        pltpu.make_async_copy(codes_ref, codes, in_sem.at[0]).start()
        pltpu.make_async_copy(scale_ref, scl, in_sem.at[1]).start()

    @pl.when(c == 0)
    def _():
        share(kc, ks)

    @pl.when(c == 1)
    def _():
        share(vc, vs)

    pltpu.make_async_copy(ln, lens, in_sem.at[2]).start()
    rloads = []
    for g in range(NX):
        for i, ref in enumerate((rk, rv)):
            rloads.append(
                pltpu.make_async_copy(
                    ref.at[0, :, pl.ds(g * HD, HD)], rsend.at[g, pl.ds(16 * i, 16)], in_sem.at[3]
                )
            )
    for cp in rloads:
        cp.start()
    loads = []
    for i, (pref, rref, dst) in enumerate(((pq, rq, qm), (pg, rg, gm), (po, ro, om))):
        for h in range(2):
            loads.append(
                pltpu.make_async_copy(
                    rref.at[0, :, pl.ds(h * HD, HD)], dst.at[pl.ds(h * RESP, RESP)], in_sem.at[4 + i]
                )
            )
            loads.append(
                pltpu.make_async_copy(
                    pref.at[:, pl.ds(h * HD, HD)], dst.at[pl.ds(RL + h * PROWS, PROWS)], in_sem.at[4 + i]
                )
            )
    for cp in loads:
        cp.start()

    pltpu.make_async_copy(kc, codes, in_sem.at[0]).wait()
    pltpu.make_async_copy(ks, scl, in_sem.at[1]).wait()
    for g in range(NX):
        for b in range(128 // SBLK):
            block = codes[b * SBLK : (b + 1) * SBLK, g * HD : (g + 1) * HD].astype(F32) * scl[b, g]
            deq[g, b * SBLK : (b + 1) * SBLK, :] = block.astype(BF)
    own_rows = pl.ds(pl.multiple_of(x * HALF, HALF), HALF)
    for half in range(2):
        table[c, zh, half, own_rows, :] = deq[x, half * HALF : (half + 1) * HALF, :]
    pltpu.make_async_copy(rsend, rsend, in_sem.at[3]).wait()

    pl.semaphore_wait(bar, len(partners))

    def psend(xt, zt, half, sem):
        src = deq.at[xt, pl.ds(pl.multiple_of(half * HALF, HALF), HALF)]
        remote(src, table.at[c, zh, half, own_rows], p_ss.at[0], sem, dev(xt, y, zt, c)).start()

    for dx in (2, 1, 3, 0):
        psend(wrap(x + dx, NX), wrap(z + 1 * sg, NZ), hy, p_rs.at[zh, x // 2])
    for dx in (2, 1, 3, 0):
        psend(wrap(x + dx, NX), wrap(z + 2 * sg, NZ), hy, p_rs.at[zh, x // 2])
    for dx in (2, 1, 3, 0):
        psend(wrap(x + dx, NX), wrap(z + 3 * sg, NZ), hy, p_rs.at[zh, x // 2])
    for dx in (2, 1, 3):
        for half in range(2):
            psend(wrap(x + dx, NX), z, half, p_rs.at[4, 0])
    rtab[p] = rsend[x]

    groups = [zh, wrap(zh + sg, NZH), wrap(zh - sg, NZH), wrap(zh + 2, NZH)]

    for i, dst in enumerate((qm, gm, om)):
        pltpu.make_async_copy(dst, dst, in_sem.at[4 + i]).wait()
    pltpu.make_async_copy(ln, lens, in_sem.at[2]).wait()
    length = lens[0]
    live = lax.broadcasted_iota(jnp.int32, (RESP, HD), 0) < length
    for h in range(2):
        block = gm[h * RESP : (h + 1) * RESP, :]
        gm[h * RESP : (h + 1) * RESP, :] = jnp.where(live, block, jnp.zeros_like(block))
    delta = jnp.sum((gm[...].astype(F32) * om[...].astype(F32)).T, axis=0, keepdims=True)

    def hand(k, part):
        remote(part, part, d_ss.at[0], d_rs.at[groups[k]], sib).start()

    def take_near():
        part = deq.at[pl.ds(0, 3)]
        remote(part, part, p_ss.at[0], p_rs.at[4, 0], sib).wait_recv()
        hand(0, table.at[c, zh])

    def take_far(k):
        zg = groups[k]
        for i in range(2):
            part = table.at[c, zg, hy, pl.ds(i * 2 * HALF, 2 * HALF)]
            remote(part, part, p_ss.at[0], p_rs.at[zg, i], sib).wait_recv()
            remote(part, part, h_ss.at[0], h_rs.at[zg, i], dev(x, wrap(y + 1 - 2 * i, NY), z, c)).start()
        hand(k, table.at[c, zg, hy])

    def take_whole(k):
        part = table.at[c, groups[k]]
        remote(part, part, p_ss.at[0], p_rs.at[groups[k], 0], sib).wait_recv()
        hand(k, part)

    def take_beside(k):
        zg = groups[k]
        for i in range(2):
            part = table.at[c, zg, 1 - hy, pl.ds(i * 2 * HALF, 2 * HALF)]
            remote(part, part, h_ss.at[0], h_rs.at[zg, i], sib).wait_recv()
        hand(k, table.at[c, zg, 1 - hy])

    def group_of(k):
        step = jnp.where(k == 1, sg, jnp.where(k == 2, -sg, jnp.where(k == 3, 2, 0)))
        return lax.rem(zh + step + 4, 4)

    def absorb(k):
        zg = group_of(k)
        other = table.at[1 - c, zg]
        remote(other, other, d_ss.at[0], d_rs.at[zg], sib).wait_recv()
        keys = table[0, zg].reshape(GROUP, HD)
        far = dot_t(keys, qm[0:RL, :])
        best = jnp.max(far, axis=0, keepdims=True)
        mx[zg, :, 0:RL] = best
        far = jnp.exp2((far - best) * (inv * LOG2E))
        sm[zg, :, 0:RL] = jnp.sum(far, axis=0, keepdims=True)
        S[zg, :, 0:RL] = far
        row = lax.broadcasted_iota(jnp.int32, (GROUP, 2 * PROWS), 0)
        lane = lax.broadcasted_iota(jnp.int32, (GROUP, 2 * PROWS), 1)
        place = ((row // HALF) % NX) * GROUP + zg * 128 + (row // 256) * HALF + row % HALF
        own = dot_t(keys, qm[RL:LANES, :])
        own = jnp.where(place <= s * PROWS + lane % PROWS, own, NEG)
        best = jnp.max(own, axis=0, keepdims=True)
        mx[zg, :, RL:LANES] = best
        own = jnp.exp2((own - best) * (inv * LOG2E))
        sm[zg, :, RL:LANES] = jnp.sum(own, axis=0, keepdims=True)
        S[zg, :, RL:LANES] = own
        DP[zg] = dot_t(table[1, zg].reshape(GROUP, HD), gm[...]) - delta

    def absorb_loop(k, _):
        absorb(k)
        return 0

    take_near()
    take_far(1)
    absorb(0)
    take_far(2)
    take_far(3)
    for k in range(1, 16):
        pt = wrap(p + k, 16)
        remote(rsend.at[pt // 4], rtab.at[p], q_ss.at[0], q_rs.at[0], (pt, s)).start()
    take_beside(1)
    take_beside(2)
    take_beside(3)
    lax.fori_loop(1, 4, absorb_loop, 0)
    part = rtab.at[pl.ds(0, 15)]
    remote(part, part, q_ss.at[0], q_rs.at[0], sib).wait_recv()
    for i in range(16):
        kr[i * 16 : (i + 1) * 16, :] = rtab[i, 0:16, :]
        vr[i * 16 : (i + 1) * 16, :] = rtab[i, 16:32, :]
    u = lax.broadcasted_iota(jnp.int32, (RESP, RESP), 0)
    t = lax.broadcasted_iota(jnp.int32, (RESP, RESP), 1)
    near = (u <= t) & (u < length)
    sr = dot_t(kr[...], qm[0:RL, :])
    tops, sums = [], []
    for h in range(2):
        part = jnp.where(near, sr[:, h * RESP : (h + 1) * RESP], NEG)
        best = jnp.max(part, axis=0, keepdims=True)
        part = jnp.exp2((part - best) * (inv * LOG2E))
        Sr[:, h * RESP : (h + 1) * RESP] = part
        tops.append(best)
        sums.append(jnp.sum(part, axis=0, keepdims=True))
    tops = jnp.concatenate(tops + [jnp.full((1, 2 * PROWS), NEG, F32)], axis=1)
    sums = jnp.concatenate(sums + [jnp.zeros((1, 2 * PROWS), F32)], axis=1)


    top = tops
    for zg in range(4):
        top = jnp.maximum(top, mx[zg])
    rscale = jnp.exp2((tops - top) * (inv * LOG2E))
    total = sums * rscale
    scales = []
    for zg in range(4):
        scale = jnp.exp2((mx[zg] - top) * (inv * LOG2E))
        total += sm[zg] * scale
        scales.append(scale)
    rtotal = 1.0 / total
    rscale = rscale * rtotal
    for zg in range(4):
        mx[zg] = scales[zg] * rtotal

    prob = Sr[...] * rscale[:, 0:RL]
    dp = dot_t(vr[...], gm[0:RL, :])
    ds = (prob * (dp - delta[:, 0:RL])).astype(BF)
    dqt[:, 0:RL] = dot_l(kr[...], ds)
    dqt[:, RL:LANES] = jnp.zeros((HD, 2 * PROWS), F32)
    dkr = (dot_n(ds, qm[0:RL, :]) * inv).astype(BF)
    dvr = dot_n(prob.astype(BF), gm[0:RL, :]).astype(BF)
    for i in range(16):
        rgs[i, 0:16, :] = dkr[i * 16 : (i + 1) * 16, :]
        rgs[i, 16:32, :] = dvr[i * 16 : (i + 1) * 16, :]
    for k in range(1, 16):
        pt = wrap(p + k, 16)
        remote(rgs.at[pt], rgr.at[p], g_ss.at[0], g_rs.at[0], (pt, s)).start()
    rgr[p] = rgs[p]

    def pair(zg, kv, i):
        rows = pl.ds(pl.multiple_of((2 * i + 1 - c) * 128, 128), 128)
        got = r1.at[kv, zg, pl.ds(i * 128, 128)]
        return remote(gout.at[kv, zg, rows], got, e_ss.at[0], e_rs.at[zg], sib)

    def ysend(zg, d):
        yt = wrap(y + d, NY)
        rows = pl.ds(pl.multiple_of(zg * 32, 32), 32)
        return remote(ady.at[yt, rows], ray.at[d, rows], ya_ss.at[0], ya_rs.at[0], dev(x, yt, z, c))

    def zsend(zt):
        return remote(adz.at[zt], raz.at[z], za_ss.at[0], za_rs.at[0], dev(x, y, zt, c))

    def spread(k):
        zg = group_of(k)
        part = gout.at[0, zg]
        remote(part, part, e_ss.at[0], e_rs.at[zg], sib).wait_recv()
        for i in range(2):
            zt = zg * 2 + i
            keep = pl.ds(pl.multiple_of((2 * i + c) * 128, 128), 128)
            got = pl.ds(i * 128, 128)
            both = gout[0, zg, keep, :].astype(F32) + r1[0, zg, got, :].astype(F32)
            both = both.astype(BF)
            rows = pl.ds(pl.multiple_of(zt * 16, 16), 16)
            for yy in range(NY):
                ady[yy, rows, :] = both[yy * 16 : (yy + 1) * 16, :]
            both = gout[1, zg, keep, :].astype(F32) + r1[1, zg, got, :].astype(F32)
            adz[zt] = both.astype(BF)
        for d in (4, 3, 5, 2, 6, 1, 7):
            ysend(zg, d).start()
        for i in range(2):
            zt = zg * 2 + i

            @pl.when(zt != z)
            def _():
                zsend(zt).start()

    def grads(k, _):
        zg = group_of(k)
        prob = S[zg] * mx[zg]
        ds = (prob * DP[zg]).astype(BF)
        dqt[...] += dot_l(table[0, zg].reshape(GROUP, HD), ds)
        for kv in range(2):
            if kv == 0:
                sums = (dot_n(ds, qm[...]) * inv).astype(BF)
            else:
                sums = dot_n(prob.astype(BF), gm[...]).astype(BF)
            for half in range(2):
                for xs in range(NX):
                    start = half * 256 + xs * HALF
                    to = xs * 128 + half * HALF
                    gout[kv, zg, to : to + HALF, :] = sums[start : start + HALF, :]
        for kv in range(2):
            for i in range(2):
                pair(zg, kv, i).start()

        if k > 0:
            spread(k - 1)

        return 0

    for k in range(4):
        grads(k, 0)

    dqs[...] = (dqt[...].T * inv).astype(BF)
    outs = []
    for h in range(2):
        outs.append(
            pltpu.make_async_copy(
                dqs.at[pl.ds(h * RESP, RESP)], o_rdq.at[0, :, pl.ds(h * HD, HD)], in_sem.at[7]
            )
        )
        outs.append(
            pltpu.make_async_copy(
                dqs.at[pl.ds(RL + h * PROWS, PROWS)], o_dq.at[:, pl.ds(h * HD, HD)], in_sem.at[7]
            )
        )
    for cp in outs:
        cp.start()

    spread(3)
    seven = ray.at[pl.ds(1, 7)]
    remote(seven, seven, ya_ss.at[0], ya_rs.at[0], sib).wait_recv()
    acc = ady[y].astype(F32)
    for d in range(1, 8):
        acc += ray[d].astype(F32)
    bdy[...] = acc.astype(BF)
    for d in range(1, 8):
        zt = wrap(z + d, NZ)
        cp = remote(
            bdy.at[pl.ds(pl.multiple_of(zt * 16, 16), 16)], rbz.at[d], zb_ss.at[0], zb_rs.at[0], dev(x, y, zt, c)
        )
        cp.start()
    remote(seven, seven, za_ss.at[0], za_rs.at[0], sib).wait_recv()
    acc = adz[z].astype(F32)
    for d in range(1, 8):
        acc += raz[wrap(z + d, NZ)].astype(F32)
    bdz[...] = acc.astype(BF)
    for d in range(1, 8):
        yt = wrap(y + d, NY)
        cp = remote(
            bdz.at[pl.ds(pl.multiple_of(yt * 16, 16), 16)], rby.at[d], yb_ss.at[0], yb_rs.at[0], dev(x, yt, z, c)
        )
        cp.start()
    some = rbz.at[pl.ds(1, 7)]
    remote(some, some, zb_ss.at[0], zb_rs.at[0], sib).wait_recv()
    acc = bdy[pl.ds(pl.multiple_of(z * 16, 16), 16), :].astype(F32)
    for d in range(1, 8):
        acc += rbz[d].astype(F32)
    fin[0:16, :] = acc.astype(BF)
    remote(some, some, yb_ss.at[0], yb_rs.at[0], sib).wait_recv()
    acc = bdz[pl.ds(pl.multiple_of(y * 16, 16), 16), :].astype(F32)
    for d in range(1, 8):
        acc += rby[d].astype(F32)
    fin[16:32, :] = acc.astype(BF)

    xo = 2 * zl + c
    zf, cf = x // 2, x % 2

    def final(i):
        zz, cc = i // 2, i % 2
        same = (xo == x) & (zl == zz) & (c == cc)
        return same, remote(fin, rfin.at[x], f_ss.at[i], f_rs.at[x], dev(xo, y, zh * 2 + zz, cc))

    for i in range(4):
        same, cp = final(i)

        @pl.when(jnp.logical_not(same))
        def _():
            cp.start()

        @pl.when(same)
        def _():
            rfin[x] = fin[...]

    part = rgr.at[pl.ds(0, 15)]
    remote(part, part, g_ss.at[0], g_rs.at[0], sib).wait_recv()
    for g in range(NX):
        acc = rgr[g * 4].astype(F32)
        for i in range(1, 4):
            acc += rgr[g * 4 + i].astype(F32)
        acc = acc.astype(BF)
        o_rdk[0, :, g * HD : (g + 1) * HD] = acc[0:16, :]
        o_rdv[0, :, g * HD : (g + 1) * HD] = acc[16:32, :]

    for xs in range(NX):
        mine = (x == xs) & (zf == zl) & (cf == c)

        @pl.when(jnp.logical_not(mine))
        def _():
            remote(fin, rfin.at[xs], f_ss.at[0], f_rs.at[xs], sib).wait_recv()

    spot = zl * 2 + c
    for xs in range(NX):
        tile = rfin[xs].astype(F32)
        for half, out in ((0, o_dk), (16, o_dv)):
            rows = tile[half : half + 4, :]
            for i in range(1, 4):
                rows = jnp.where(spot == i, tile[half + 4 * i : half + 4 * i + 4, :], rows)
            out[:, xs * HD : (xs + 1) * HD] = rows.astype(BF)

    for i in range(4):
        same, cp = final(i)

        @pl.when(jnp.logical_not(same))
        def _():
            cp.wait_send()

    def sent(part, sem):
        remote(part, part, sem.at[0], p_rs.at[0, 0], sib).wait_send()

    sent(gout.at[0, pl.ds(0, 3), pl.ds(0, 384)], p_ss)
    sent(rtab.at[pl.ds(0, 15)], q_ss)
    sent(gout.at[0, pl.ds(0, 3), pl.ds(0, 256)], h_ss)
    sent(table.at[0], d_ss)
    sent(gout.at[0], e_ss)
    sent(seven, ya_ss)
    sent(seven, za_ss)
    sent(some, yb_ss)
    sent(some, zb_ss)
    sent(rtab.at[pl.ds(0, 15)], g_ss)
    pltpu.make_async_copy(dqs, dqs, in_sem.at[7]).wait()


def place(*refs):
    for i in range(6):
        refs[6 + i][...] = refs[i][...]


def shards(*args):
    hbm = pl.BlockSpec(memory_space=pl.ANY)
    vmem = pl.BlockSpec(memory_space=pltpu.VMEM)
    dma = pltpu.SemaphoreType.DMA
    shape = jax.ShapeDtypeStruct
    made = pl.pallas_call(
        kernel,
        out_shape=(
            shape((PROWS, 256), BF),
            shape((4, 512), BF),
            shape((4, 512), BF),
            shape((1, RESP, 256), BF),
            shape((1, 16, 512), BF),
            shape((1, 16, 512), BF),
        ),
        in_specs=[hbm] * 13,
        out_specs=(hbm, vmem, vmem, hbm, vmem, vmem),
        scratch_shapes=[
            pltpu.VMEM((LANES, HD), BF),
            pltpu.VMEM((LANES, HD), BF),
            pltpu.VMEM((LANES, HD), BF),
            pltpu.VMEM((128, 512), BF),
            pltpu.VMEM((4, 128, HD), BF),
            pltpu.VMEM((2, 4, 2, GROUP // 2, HD), BF),
            pltpu.VMEM((4, 32, HD), BF),
            pltpu.VMEM((16, 32, HD), BF),
            pltpu.VMEM((RESP, HD), BF),
            pltpu.VMEM((RESP, HD), BF),
            pltpu.VMEM((4, GROUP, LANES), F32),
            pltpu.VMEM((4, GROUP, LANES), F32),
            pltpu.VMEM((RESP, RL), F32),
            pltpu.VMEM((LANES, HD), BF),
            pltpu.VMEM((HD, LANES), F32),
            pltpu.VMEM((4, 1, LANES), F32),
            pltpu.VMEM((4, 1, LANES), F32),
            pltpu.VMEM((2, 4, GROUP, HD), BF),
            pltpu.VMEM((2, 4, 256, HD), BF),
            pltpu.VMEM((8, 128, HD), BF),
            pltpu.VMEM((8, 128, HD), BF),
            pltpu.VMEM((8, 128, HD), BF),
            pltpu.VMEM((8, 128, HD), BF),
            pltpu.VMEM((128, HD), BF),
            pltpu.VMEM((128, HD), BF),
            pltpu.VMEM((8, 16, HD), BF),
            pltpu.VMEM((8, 16, HD), BF),
            pltpu.VMEM((32, HD), BF),
            pltpu.VMEM((4, 32, HD), BF),
            pltpu.VMEM((16, 32, HD), BF),
            pltpu.VMEM((16, 32, HD), BF),
            pltpu.SMEM((4, 4), F32),
            pltpu.SMEM((1,), jnp.int32),
            dma((8,)),
            dma((1,)),
            dma((5, 2)),
            dma((1,)),
            dma((1,)),
            dma((1,)),
            dma((4, 2)),
            dma((1,)),
            dma((4,)),
            dma((1,)),
            dma((4,)),
        ]
        + [dma((1,))] * 8
        + [dma((4,)), dma((4,)), dma((1,)), dma((1,))],
        compiler_params=pltpu.CompilerParams(
            collective_id=0, has_side_effects=True, vmem_limit_bytes=60 * 1024 * 1024
        ),
        name="attention_backward",
    )(*args)
    return pl.pallas_call(
        place,
        out_shape=tuple(shape(a.shape, a.dtype) for a in made),
        in_specs=[vmem] * 6,
        out_specs=[vmem] * 6,
        compiler_params=pltpu.CompilerParams(vmem_limit_bytes=60 * 1024 * 1024),
        name="place_outputs",
    )(*made)


def solution(mesh):
    wide = P("sample", "prompt")
    block = P("prompt", None)
    resp = P("sample", None, "prompt")
    near = P("sample", "prompt", None)
    owned = P(("prompt", "sample"), None)
    return jax.shard_map(
        shards,
        mesh=mesh,
        in_specs=(wide, wide, wide, block, block, block, block, resp, resp, resp, near, near, P("sample")),
        out_specs=(wide, owned, owned, resp, near, near),
        check_vma=False,
    )
```

```python
import math

import jax
import jax.numpy as jnp
from jax import lax
from jax.experimental import pallas as pl
from jax.experimental.pallas import tpu as pltpu
from jax.sharding import PartitionSpec as P

HD = 128
SBLK = 32
MESH = pl.DeviceIdType.MESH
NEG = -1e30
F32 = jnp.float32
BF = jnp.bfloat16
LOG2E = 1.4426950408889634

NX, NY, NZ, NZH = 4, 8, 8, 4
RESP = 256
PROWS = 64
RL = 2 * RESP
LANES = RL + 2 * PROWS
GROUP = 512
HALF = 64


def dot_t(a, b):
    return lax.dot_general(a, b, (((1,), (1,)), ((), ())), preferred_element_type=F32)


def dot_n(a, b):
    return lax.dot_general(a, b, (((1,), (0,)), ((), ())), preferred_element_type=F32)


def dot_l(a, b):
    return lax.dot_general(a, b, (((0,), (0,)), ((), ())), preferred_element_type=F32)


def kernel(
    pq, pg, po, kc, vc, ks, vs, rq, rg, ro, rk, rv, ln,
    o_dq, o_dk, o_dv, o_rdq, o_rdk, o_rdv,
    qm, gm, om, codes, deq, table, rsend, rtab, kr, vr, S, DP, Sr, dqt,
    mx, sm, gout, r1, ady, adz, ray, raz, bdy, bdz, rby, rbz, fin, rfin, rgs, rgr, scl, lens,
    in_sem,
    p_ss, p_rs, q_ss, q_rs, h_ss, h_rs, d_ss, d_rs, e_ss, e_rs, ya_ss, ya_rs, za_ss, za_rs,
    yb_ss, yb_rs, zb_ss, zb_rs, f_ss, f_rs, g_ss, g_rs,
):
    p = lax.axis_index("prompt")
    s = lax.axis_index("sample")
    x, zh = p // 4, p % 4
    y, zl, c = s // 4, (s // 2) % 2, s % 2
    z = zh * 2 + zl
    sg = 2 * zl - 1
    hy = y % 2
    inv = 1.0 / math.sqrt(HD)

    def dev(xx, yy, zz, cc):
        return (xx * 4 + zz // 2, yy * 4 + (zz % 2) * 2 + cc)

    def wrap(v, n):
        return lax.rem(v + 2 * n, n)

    def remote(src, dst, ss, rs, to):
        return pltpu.make_async_remote_copy(src, dst, ss, rs, device_id=to, device_id_type=MESH)

    sib = dev(x, y, z, 1 - c)

    bar = pltpu.get_barrier_semaphore()
    partners = []
    for dx in range(NX):
        for dz in range(NZ):
            if dx or dz:
                partners.append(dev(wrap(x + dx, NX), y, wrap(z + dz, NZ), c))
    for dy in range(1, NY):
        partners.append(dev(x, wrap(y + dy, NY), z, c))
    for dx in range(NX):
        for zz in range(2):
            partners.append(dev(wrap(x + dx, NX), y, zh * 2 + zz, 1 - c))
    for to in partners:
        pl.semaphore_signal(bar, inc=1, device_id=to, device_id_type=MESH)

    def share(codes_ref, scale_ref):
        pltpu.make_async_copy(codes_ref, codes, in_sem.at[0]).start()
        pltpu.make_async_copy(scale_ref, scl, in_sem.at[1]).start()

    @pl.when(c == 0)
    def _():
        share(kc, ks)

    @pl.when(c == 1)
    def _():
        share(vc, vs)

    pltpu.make_async_copy(ln, lens, in_sem.at[2]).start()
    rloads = []
    for g in range(NX):
        for i, ref in enumerate((rk, rv)):
            rloads.append(
                pltpu.make_async_copy(
                    ref.at[0, :, pl.ds(g * HD, HD)], rsend.at[g, pl.ds(16 * i, 16)], in_sem.at[3]
                )
            )
    for cp in rloads:
        cp.start()
    loads = []
    for i, (pref, rref, dst) in enumerate(((pq, rq, qm), (pg, rg, gm), (po, ro, om))):
        for h in range(2):
            loads.append(
                pltpu.make_async_copy(
                    rref.at[0, :, pl.ds(h * HD, HD)], dst.at[pl.ds(h * RESP, RESP)], in_sem.at[4 + i]
                )
            )
            loads.append(
                pltpu.make_async_copy(
                    pref.at[:, pl.ds(h * HD, HD)], dst.at[pl.ds(RL + h * PROWS, PROWS)], in_sem.at[4 + i]
                )
            )
    for cp in loads:
        cp.start()

    pltpu.make_async_copy(kc, codes, in_sem.at[0]).wait()
    pltpu.make_async_copy(ks, scl, in_sem.at[1]).wait()
    for g in range(NX):
        for b in range(128 // SBLK):
            block = codes[b * SBLK : (b + 1) * SBLK, g * HD : (g + 1) * HD].astype(F32) * scl[b, g]
            deq[g, b * SBLK : (b + 1) * SBLK, :] = block.astype(BF)
    own_rows = pl.ds(pl.multiple_of(x * HALF, HALF), HALF)
    for half in range(2):
        table[c, zh, half, own_rows, :] = deq[x, half * HALF : (half + 1) * HALF, :]
    pltpu.make_async_copy(rsend, rsend, in_sem.at[3]).wait()

    pl.semaphore_wait(bar, len(partners))

    def psend(xt, zt, half, sem):
        src = deq.at[xt, pl.ds(pl.multiple_of(half * HALF, HALF), HALF)]
        remote(src, table.at[c, zh, half, own_rows], p_ss.at[0], sem, dev(xt, y, zt, c)).start()

    for dx in (2, 1, 3, 0):
        psend(wrap(x + dx, NX), wrap(z + 1 * sg, NZ), hy, p_rs.at[zh, x // 2])
    for dx in (2, 1, 3, 0):
        psend(wrap(x + dx, NX), wrap(z + 2 * sg, NZ), hy, p_rs.at[zh, x // 2])
    for dx in (2, 1, 3, 0):
        psend(wrap(x + dx, NX), wrap(z + 3 * sg, NZ), hy, p_rs.at[zh, x // 2])
    for dx in (2, 1, 3):
        for half in range(2):
            psend(wrap(x + dx, NX), z, half, p_rs.at[4, 0])
    rtab[p] = rsend[x]

    groups = [zh, wrap(zh + sg, NZH), wrap(zh - sg, NZH), wrap(zh + 2, NZH)]

    for i, dst in enumerate((qm, gm, om)):
        pltpu.make_async_copy(dst, dst, in_sem.at[4 + i]).wait()
    pltpu.make_async_copy(ln, lens, in_sem.at[2]).wait()
    length = lens[0]
    live = lax.broadcasted_iota(jnp.int32, (RESP, HD), 0) < length
    for h in range(2):
        block = gm[h * RESP : (h + 1) * RESP, :]
        gm[h * RESP : (h + 1) * RESP, :] = jnp.where(live, block, jnp.zeros_like(block))
    delta = jnp.sum((gm[...].astype(F32) * om[...].astype(F32)).T, axis=0, keepdims=True)

    def hand(k, part):
        remote(part, part, d_ss.at[0], d_rs.at[groups[k]], sib).start()

    def take_near():
        part = deq.at[pl.ds(0, 3)]
        remote(part, part, p_ss.at[0], p_rs.at[4, 0], sib).wait_recv()
        hand(0, table.at[c, zh])

    def take_far(k):
        zg = groups[k]
        for i in range(2):
            part = table.at[c, zg, hy, pl.ds(i * 2 * HALF, 2 * HALF)]
            remote(part, part, p_ss.at[0], p_rs.at[zg, i], sib).wait_recv()
            remote(part, part, h_ss.at[0], h_rs.at[zg, i], dev(x, wrap(y + 1 - 2 * i, NY), z, c)).start()
        hand(k, table.at[c, zg, hy])

    def take_whole(k):
        part = table.at[c, groups[k]]
        remote(part, part, p_ss.at[0], p_rs.at[groups[k], 0], sib).wait_recv()
        hand(k, part)

    def take_beside(k):
        zg = groups[k]
        for i in range(2):
            part = table.at[c, zg, 1 - hy, pl.ds(i * 2 * HALF, 2 * HALF)]
            remote(part, part, h_ss.at[0], h_rs.at[zg, i], sib).wait_recv()
        hand(k, table.at[c, zg, 1 - hy])

    def group_of(k):
        step = jnp.where(k == 1, sg, jnp.where(k == 2, -sg, jnp.where(k == 3, 2, 0)))
        return lax.rem(zh + step + 4, 4)

    def absorb(k):
        zg = group_of(k)
        other = table.at[1 - c, zg]
        remote(other, other, d_ss.at[0], d_rs.at[zg], sib).wait_recv()
        keys = table[0, zg].reshape(GROUP, HD)
        far = dot_t(keys, qm[0:RL, :])
        best = jnp.max(far, axis=0, keepdims=True)
        mx[zg, :, 0:RL] = best
        far = jnp.exp2((far - best) * (inv * LOG2E))
        sm[zg, :, 0:RL] = jnp.sum(far, axis=0, keepdims=True)
        S[zg, :, 0:RL] = far
        row = lax.broadcasted_iota(jnp.int32, (GROUP, 2 * PROWS), 0)
        lane = lax.broadcasted_iota(jnp.int32, (GROUP, 2 * PROWS), 1)
        place = ((row // HALF) % NX) * GROUP + zg * 128 + (row // 256) * HALF + row % HALF
        own = dot_t(keys, qm[RL:LANES, :])
        own = jnp.where(place <= s * PROWS + lane % PROWS, own, NEG)
        best = jnp.max(own, axis=0, keepdims=True)
        mx[zg, :, RL:LANES] = best
        own = jnp.exp2((own - best) * (inv * LOG2E))
        sm[zg, :, RL:LANES] = jnp.sum(own, axis=0, keepdims=True)
        S[zg, :, RL:LANES] = own
        DP[zg] = dot_t(table[1, zg].reshape(GROUP, HD), gm[...]) - delta

    def absorb_loop(k, _):
        absorb(k)
        return 0

    take_near()
    take_far(1)
    absorb(0)
    take_far(2)
    take_far(3)
    for k in range(1, 16):
        pt = wrap(p + k, 16)
        remote(rsend.at[pt // 4], rtab.at[p], q_ss.at[0], q_rs.at[0], (pt, s)).start()
    take_beside(1)
    take_beside(2)
    take_beside(3)
    lax.fori_loop(1, 4, absorb_loop, 0)
    part = rtab.at[pl.ds(0, 15)]
    remote(part, part, q_ss.at[0], q_rs.at[0], sib).wait_recv()
    for i in range(16):
        kr[i * 16 : (i + 1) * 16, :] = rtab[i, 0:16, :]
        vr[i * 16 : (i + 1) * 16, :] = rtab[i, 16:32, :]
    u = lax.broadcasted_iota(jnp.int32, (RESP, RESP), 0)
    t = lax.broadcasted_iota(jnp.int32, (RESP, RESP), 1)
    near = (u <= t) & (u < length)
    sr = dot_t(kr[...], qm[0:RL, :])
    tops, sums = [], []
    for h in range(2):
        part = jnp.where(near, sr[:, h * RESP : (h + 1) * RESP], NEG)
        best = jnp.max(part, axis=0, keepdims=True)
        part = jnp.exp2((part - best) * (inv * LOG2E))
        Sr[:, h * RESP : (h + 1) * RESP] = part
        tops.append(best)
        sums.append(jnp.sum(part, axis=0, keepdims=True))
    tops = jnp.concatenate(tops + [jnp.full((1, 2 * PROWS), NEG, F32)], axis=1)
    sums = jnp.concatenate(sums + [jnp.zeros((1, 2 * PROWS), F32)], axis=1)


    top = tops
    for zg in range(4):
        top = jnp.maximum(top, mx[zg])
    rscale = jnp.exp2((tops - top) * (inv * LOG2E))
    total = sums * rscale
    scales = []
    for zg in range(4):
        scale = jnp.exp2((mx[zg] - top) * (inv * LOG2E))
        total += sm[zg] * scale
        scales.append(scale)
    rtotal = 1.0 / total
    rscale = rscale * rtotal
    for zg in range(4):
        mx[zg] = scales[zg] * rtotal

    prob = Sr[...] * rscale[:, 0:RL]
    dp = dot_t(vr[...], gm[0:RL, :])
    ds = (prob * (dp - delta[:, 0:RL])).astype(BF)
    dqt[:, 0:RL] = dot_l(kr[...], ds)
    dqt[:, RL:LANES] = jnp.zeros((HD, 2 * PROWS), F32)
    dkr = (dot_n(ds, qm[0:RL, :]) * inv).astype(BF)
    dvr = dot_n(prob.astype(BF), gm[0:RL, :]).astype(BF)
    for i in range(16):
        rgs[i, 0:16, :] = dkr[i * 16 : (i + 1) * 16, :]
        rgs[i, 16:32, :] = dvr[i * 16 : (i + 1) * 16, :]
    for k in range(1, 16):
        pt = wrap(p + k, 16)
        remote(rgs.at[pt], rgr.at[p], g_ss.at[0], g_rs.at[0], (pt, s)).start()
    rgr[p] = rgs[p]

    def pair(zg, kv, i):
        rows = pl.ds(pl.multiple_of((2 * i + 1 - c) * 128, 128), 128)
        got = r1.at[kv, zg, pl.ds(i * 128, 128)]
        return remote(gout.at[kv, zg, rows], got, e_ss.at[0], e_rs.at[zg], sib)

    def ysend(zg, d):
        yt = wrap(y + d, NY)
        rows = pl.ds(pl.multiple_of(zg * 32, 32), 32)
        return remote(ady.at[yt, rows], ray.at[d, rows], ya_ss.at[0], ya_rs.at[0], dev(x, yt, z, c))

    def zsend(zt):
        return remote(adz.at[zt], raz.at[z], za_ss.at[0], za_rs.at[0], dev(x, y, zt, c))

    def spread(k):
        zg = group_of(k)
        part = gout.at[0, zg]
        remote(part, part, e_ss.at[0], e_rs.at[zg], sib).wait_recv()
        for i in range(2):
            zt = zg * 2 + i
            keep = pl.ds(pl.multiple_of((2 * i + c) * 128, 128), 128)
            got = pl.ds(i * 128, 128)
            both = gout[0, zg, keep, :].astype(F32) + r1[0, zg, got, :].astype(F32)
            both = both.astype(BF)
            rows = pl.ds(pl.multiple_of(zt * 16, 16), 16)
            for yy in range(NY):
                ady[yy, rows, :] = both[yy * 16 : (yy + 1) * 16, :]
            both = gout[1, zg, keep, :].astype(F32) + r1[1, zg, got, :].astype(F32)
            adz[zt] = both.astype(BF)
        for d in (4, 3, 5, 2, 6, 1, 7):
            ysend(zg, d).start()
        for i in range(2):
            zt = zg * 2 + i

            @pl.when(zt != z)
            def _():
                zsend(zt).start()

    def grads(k, _):
        zg = group_of(k)
        prob = S[zg] * mx[zg]
        ds = (prob * DP[zg]).astype(BF)
        dqt[...] += dot_l(table[0, zg].reshape(GROUP, HD), ds)
        for kv in range(2):
            if kv == 0:
                sums = (dot_n(ds, qm[...]) * inv).astype(BF)
            else:
                sums = dot_n(prob.astype(BF), gm[...]).astype(BF)
            for half in range(2):
                for xs in range(NX):
                    start = half * 256 + xs * HALF
                    to = xs * 128 + half * HALF
                    gout[kv, zg, to : to + HALF, :] = sums[start : start + HALF, :]
        for kv in range(2):
            for i in range(2):
                pair(zg, kv, i).start()

        if k > 0:
            spread(k - 1)

        return 0

    for k in range(4):
        grads(k, 0)

    dqs = (dqt[...].T * inv).astype(BF)
    for h in range(2):
        o_rdq[0, :, h * HD : (h + 1) * HD] = dqs[h * RESP : (h + 1) * RESP, :]
        o_dq[:, h * HD : (h + 1) * HD] = dqs[RL + h * PROWS : RL + (h + 1) * PROWS, :]

    spread(3)
    seven = ray.at[pl.ds(1, 7)]
    remote(seven, seven, ya_ss.at[0], ya_rs.at[0], sib).wait_recv()
    acc = ady[y].astype(F32)
    for d in range(1, 8):
        acc += ray[d].astype(F32)
    bdy[...] = acc.astype(BF)
    for d in range(1, 8):
        zt = wrap(z + d, NZ)
        cp = remote(
            bdy.at[pl.ds(pl.multiple_of(zt * 16, 16), 16)], rbz.at[d], zb_ss.at[0], zb_rs.at[0], dev(x, y, zt, c)
        )
        cp.start()
    remote(seven, seven, za_ss.at[0], za_rs.at[0], sib).wait_recv()
    acc = adz[z].astype(F32)
    for d in range(1, 8):
        acc += raz[wrap(z + d, NZ)].astype(F32)
    bdz[...] = acc.astype(BF)
    for d in range(1, 8):
        yt = wrap(y + d, NY)
        cp = remote(
            bdz.at[pl.ds(pl.multiple_of(yt * 16, 16), 16)], rby.at[d], yb_ss.at[0], yb_rs.at[0], dev(x, yt, z, c)
        )
        cp.start()
    some = rbz.at[pl.ds(1, 7)]
    remote(some, some, zb_ss.at[0], zb_rs.at[0], sib).wait_recv()
    acc = bdy[pl.ds(pl.multiple_of(z * 16, 16), 16), :].astype(F32)
    for d in range(1, 8):
        acc += rbz[d].astype(F32)
    fin[0:16, :] = acc.astype(BF)
    remote(some, some, yb_ss.at[0], yb_rs.at[0], sib).wait_recv()
    acc = bdz[pl.ds(pl.multiple_of(y * 16, 16), 16), :].astype(F32)
    for d in range(1, 8):
        acc += rby[d].astype(F32)
    fin[16:32, :] = acc.astype(BF)

    xo = 2 * zl + c
    zf, cf = x // 2, x % 2

    def final(i):
        zz, cc = i // 2, i % 2
        same = (xo == x) & (zl == zz) & (c == cc)
        return same, remote(fin, rfin.at[x], f_ss.at[i], f_rs.at[x], dev(xo, y, zh * 2 + zz, cc))

    for i in range(4):
        same, cp = final(i)

        @pl.when(jnp.logical_not(same))
        def _():
            cp.start()

        @pl.when(same)
        def _():
            rfin[x] = fin[...]

    part = rgr.at[pl.ds(0, 15)]
    remote(part, part, g_ss.at[0], g_rs.at[0], sib).wait_recv()
    for g in range(NX):
        acc = rgr[g * 4].astype(F32)
        for i in range(1, 4):
            acc += rgr[g * 4 + i].astype(F32)
        acc = acc.astype(BF)
        o_rdk[0, :, g * HD : (g + 1) * HD] = acc[0:16, :]
        o_rdv[0, :, g * HD : (g + 1) * HD] = acc[16:32, :]

    for xs in range(NX):
        mine = (x == xs) & (zf == zl) & (cf == c)

        @pl.when(jnp.logical_not(mine))
        def _():
            remote(fin, rfin.at[xs], f_ss.at[0], f_rs.at[xs], sib).wait_recv()

    spot = zl * 2 + c
    for xs in range(NX):
        tile = rfin[xs].astype(F32)
        for half, out in ((0, o_dk), (16, o_dv)):
            rows = tile[half : half + 4, :]
            for i in range(1, 4):
                rows = jnp.where(spot == i, tile[half + 4 * i : half + 4 * i + 4, :], rows)
            out[:, xs * HD : (xs + 1) * HD] = rows.astype(BF)

    for i in range(4):
        same, cp = final(i)

        @pl.when(jnp.logical_not(same))
        def _():
            cp.wait_send()

    def sent(part, sem):
        remote(part, part, sem.at[0], p_rs.at[0, 0], sib).wait_send()

    sent(gout.at[0, pl.ds(0, 3), pl.ds(0, 384)], p_ss)
    sent(rtab.at[pl.ds(0, 15)], q_ss)
    sent(gout.at[0, pl.ds(0, 3), pl.ds(0, 256)], h_ss)
    sent(table.at[0], d_ss)
    sent(gout.at[0], e_ss)
    sent(seven, ya_ss)
    sent(seven, za_ss)
    sent(some, yb_ss)
    sent(some, zb_ss)
    sent(rtab.at[pl.ds(0, 15)], g_ss)


def place(*refs):
    for i in range(6):
        refs[6 + i][...] = refs[i][...]


def shards(*args):
    hbm = pl.BlockSpec(memory_space=pltpu.HBM)
    vmem = pl.BlockSpec(memory_space=pltpu.VMEM)
    dma = pltpu.SemaphoreType.DMA
    shape = jax.ShapeDtypeStruct
    made = pl.pallas_call(
        kernel,
        out_shape=(
            pltpu.VMEM((PROWS, 256), BF),
            pltpu.VMEM((4, 512), BF),
            pltpu.VMEM((4, 512), BF),
            pltpu.VMEM((1, RESP, 256), BF),
            pltpu.VMEM((1, 16, 512), BF),
            pltpu.VMEM((1, 16, 512), BF),
        ),
        in_specs=[hbm] * 13,
        out_specs=[vmem] * 6,
        scratch_shapes=[
            pltpu.VMEM((LANES, HD), BF),
            pltpu.VMEM((LANES, HD), BF),
            pltpu.VMEM((LANES, HD), BF),
            pltpu.VMEM((128, 512), BF),
            pltpu.VMEM((4, 128, HD), BF),
            pltpu.VMEM((2, 4, 2, GROUP // 2, HD), BF),
            pltpu.VMEM((4, 32, HD), BF),
            pltpu.VMEM((16, 32, HD), BF),
            pltpu.VMEM((RESP, HD), BF),
            pltpu.VMEM((RESP, HD), BF),
            pltpu.VMEM((4, GROUP, LANES), F32),
            pltpu.VMEM((4, GROUP, LANES), F32),
            pltpu.VMEM((RESP, RL), F32),
            pltpu.VMEM((HD, LANES), F32),
            pltpu.VMEM((4, 1, LANES), F32),
            pltpu.VMEM((4, 1, LANES), F32),
            pltpu.VMEM((2, 4, GROUP, HD), BF),
            pltpu.VMEM((2, 4, 256, HD), BF),
            pltpu.VMEM((8, 128, HD), BF),
            pltpu.VMEM((8, 128, HD), BF),
            pltpu.VMEM((8, 128, HD), BF),
            pltpu.VMEM((8, 128, HD), BF),
            pltpu.VMEM((128, HD), BF),
            pltpu.VMEM((128, HD), BF),
            pltpu.VMEM((8, 16, HD), BF),
            pltpu.VMEM((8, 16, HD), BF),
            pltpu.VMEM((32, HD), BF),
            pltpu.VMEM((4, 32, HD), BF),
            pltpu.VMEM((16, 32, HD), BF),
            pltpu.VMEM((16, 32, HD), BF),
            pltpu.SMEM((4, 4), F32),
            pltpu.SMEM((1,), jnp.int32),
            dma((7,)),
            dma((1,)),
            dma((5, 2)),
            dma((1,)),
            dma((1,)),
            dma((1,)),
            dma((4, 2)),
            dma((1,)),
            dma((4,)),
            dma((1,)),
            dma((4,)),
        ]
        + [dma((1,))] * 8
        + [dma((4,)), dma((4,)), dma((1,)), dma((1,))],
        compiler_params=pltpu.CompilerParams(
            collective_id=0, has_side_effects=True, vmem_limit_bytes=61440 * 1024
        ),
        name="attention_backward",
    )(*args)
    return pl.pallas_call(
        place,
        out_shape=tuple(shape(a.shape, BF) for a in made),
        in_specs=[vmem] * 6,
        out_specs=[vmem] * 6,
        compiler_params=pltpu.CompilerParams(vmem_limit_bytes=40 * 1024 * 1024),
        name="place_outputs",
    )(*made)


def solution(mesh):
    wide = P("sample", "prompt")
    block = P("prompt", None)
    resp = P("sample", None, "prompt")
    near = P("sample", "prompt", None)
    owned = P(("prompt", "sample"), None)
    return jax.shard_map(
        shards,
        mesh=mesh,
        in_specs=(wide, wide, wide, block, block, block, block, resp, resp, resp, near, near, P("sample")),
        out_specs=(wide, owned, owned, resp, near, near),
        check_vma=False,
    )
```

```python
import math

import jax
import jax.numpy as jnp
from jax import lax
from jax.experimental import pallas as pl
from jax.experimental.pallas import tpu as pltpu
from jax.sharding import PartitionSpec as P

HD = 128
SBLK = 32
MESH = pl.DeviceIdType.MESH
NEG = -1e30
F32 = jnp.float32
BF = jnp.bfloat16
LOG2E = 1.4426950408889634

NX, NY, NZ, NZH = 4, 8, 8, 4
RESP = 256
PROWS = 64
RL = 2 * RESP
LANES = RL + 2 * PROWS
GROUP = 512
HALF = 64


def dot_t(a, b):
    return lax.dot_general(a, b, (((1,), (1,)), ((), ())), preferred_element_type=F32)


def dot_n(a, b):
    return lax.dot_general(a, b, (((1,), (0,)), ((), ())), preferred_element_type=F32)


def dot_l(a, b):
    return lax.dot_general(a, b, (((0,), (0,)), ((), ())), preferred_element_type=F32)


def kernel(
    pq, pg, po, kc, vc, ks, vs, rq, rg, ro, rk, rv, ln,
    o_dq, o_dk, o_dv, o_rdq, o_rdk, o_rdv,
    qm, gm, om, codes, deq, table, rsend, rtab, kr, vr, S, DP, Sr, dqt,
    mx, sm, gout, r1, ady, adz, ray, raz, bdy, bdz, rby, rbz, fin, rfin, rgs, rgr, scl, lens,
    in_sem,
    p_ss, p_rs, q_ss, q_rs, h_ss, h_rs, d_ss, d_rs, e_ss, e_rs, ya_ss, ya_rs, za_ss, za_rs,
    yb_ss, yb_rs, zb_ss, zb_rs, f_ss, f_rs, g_ss, g_rs,
):
    p = lax.axis_index("prompt")
    s = lax.axis_index("sample")
    x, zh = p // 4, p % 4
    y, zl, c = s // 4, (s // 2) % 2, s % 2
    z = zh * 2 + zl
    sg = 2 * zl - 1
    hy = y % 2
    inv = 1.0 / math.sqrt(HD)

    def dev(xx, yy, zz, cc):
        return (xx * 4 + zz // 2, yy * 4 + (zz % 2) * 2 + cc)

    def wrap(v, n):
        return lax.rem(v + 2 * n, n)

    def remote(src, dst, ss, rs, to):
        return pltpu.make_async_remote_copy(src, dst, ss, rs, device_id=to, device_id_type=MESH)

    sib = dev(x, y, z, 1 - c)

    bar = pltpu.get_barrier_semaphore()
    partners = []
    for dx in range(NX):
        for dz in (0, 1, 2, 3, 4, 6) if dx else range(1, NZ):
            partners.append(dev(wrap(x + dx, NX), y, wrap(z + sg * dz, NZ), c))
    for dy in range(1, NY):
        partners.append(dev(x, wrap(y + dy, NY), z, c))
    for dx in range(NX):
        for zz in range(2):
            partners.append(dev(wrap(x + dx, NX), y, zh * 2 + zz, 1 - c))
    for to in partners:
        pl.semaphore_signal(bar, inc=1, device_id=to, device_id_type=MESH)

    def share(codes_ref, scale_ref):
        pltpu.make_async_copy(codes_ref, codes, in_sem.at[0]).start()
        pltpu.make_async_copy(scale_ref, scl, in_sem.at[1]).start()

    @pl.when(c == 0)
    def _():
        share(kc, ks)

    @pl.when(c == 1)
    def _():
        share(vc, vs)

    pltpu.make_async_copy(ln, lens, in_sem.at[2]).start()
    rloads = []
    for g in range(NX):
        for i, ref in enumerate((rk, rv)):
            rloads.append(
                pltpu.make_async_copy(
                    ref.at[0, :, pl.ds(g * HD, HD)], rsend.at[g, pl.ds(16 * i, 16)], in_sem.at[3]
                )
            )
    for cp in rloads:
        cp.start()
    loads = []
    for i, (pref, rref, dst) in enumerate(((pq, rq, qm), (pg, rg, gm), (po, ro, om))):
        for h in range(2):
            loads.append(
                pltpu.make_async_copy(
                    rref.at[0, :, pl.ds(h * HD, HD)], dst.at[pl.ds(h * RESP, RESP)], in_sem.at[4 + i]
                )
            )
            loads.append(
                pltpu.make_async_copy(
                    pref.at[:, pl.ds(h * HD, HD)], dst.at[pl.ds(RL + h * PROWS, PROWS)], in_sem.at[4 + i]
                )
            )
    for cp in loads:
        cp.start()

    pltpu.make_async_copy(kc, codes, in_sem.at[0]).wait()
    pltpu.make_async_copy(ks, scl, in_sem.at[1]).wait()
    for g in range(NX):
        for b in range(128 // SBLK):
            block = codes[b * SBLK : (b + 1) * SBLK, g * HD : (g + 1) * HD].astype(F32) * scl[b, g]
            deq[g, b * SBLK : (b + 1) * SBLK, :] = block.astype(BF)
    own_rows = pl.ds(pl.multiple_of(x * HALF, HALF), HALF)
    for half in range(2):
        table[c, zh, half, own_rows, :] = deq[x, half * HALF : (half + 1) * HALF, :]
    pltpu.make_async_copy(rsend, rsend, in_sem.at[3]).wait()

    pl.semaphore_wait(bar, len(partners))

    def psend(xt, zt, half, sem):
        src = deq.at[xt, pl.ds(pl.multiple_of(half * HALF, HALF), HALF)]
        remote(src, table.at[c, zh, half, own_rows], p_ss.at[0], sem, dev(xt, y, zt, c)).start()

    for dx in (2, 1, 3, 0):
        psend(wrap(x + dx, NX), wrap(z + 1 * sg, NZ), hy, p_rs.at[zh, x // 2])
    for dx in (2, 1, 3, 0):
        psend(wrap(x + dx, NX), wrap(z + 2 * sg, NZ), hy, p_rs.at[zh, x // 2])
    for dx in (2, 1, 3, 0):
        psend(wrap(x + dx, NX), wrap(z + 3 * sg, NZ), hy, p_rs.at[zh, x // 2])
    for dx in (2, 1, 3):
        for half in range(2):
            psend(wrap(x + dx, NX), z, half, p_rs.at[4, 0])
    rtab[p] = rsend[x]

    groups = [zh, wrap(zh + sg, NZH), wrap(zh - sg, NZH), wrap(zh + 2, NZH)]

    for i, dst in enumerate((qm, gm, om)):
        pltpu.make_async_copy(dst, dst, in_sem.at[4 + i]).wait()
    pltpu.make_async_copy(ln, lens, in_sem.at[2]).wait()
    length = lens[0]
    live = lax.broadcasted_iota(jnp.int32, (RESP, HD), 0) < length
    for h in range(2):
        block = gm[h * RESP : (h + 1) * RESP, :]
        gm[h * RESP : (h + 1) * RESP, :] = jnp.where(live, block, jnp.zeros_like(block))
    delta = jnp.sum((gm[...].astype(F32) * om[...].astype(F32)).T, axis=0, keepdims=True)

    def hand(k, part):
        remote(part, part, d_ss.at[0], d_rs.at[groups[k]], sib).start()

    def take_near():
        part = deq.at[pl.ds(0, 3)]
        remote(part, part, p_ss.at[0], p_rs.at[4, 0], sib).wait_recv()
        hand(0, table.at[c, zh])

    def take_far(k):
        zg = groups[k]
        for i in range(2):
            part = table.at[c, zg, hy, pl.ds(i * 2 * HALF, 2 * HALF)]
            remote(part, part, p_ss.at[0], p_rs.at[zg, i], sib).wait_recv()
            remote(part, part, h_ss.at[0], h_rs.at[zg, i], dev(x, wrap(y + 1 - 2 * i, NY), z, c)).start()
        hand(k, table.at[c, zg, hy])

    def take_whole(k):
        part = table.at[c, groups[k]]
        remote(part, part, p_ss.at[0], p_rs.at[groups[k], 0], sib).wait_recv()
        hand(k, part)

    def take_beside(k):
        zg = groups[k]
        for i in range(2):
            part = table.at[c, zg, 1 - hy, pl.ds(i * 2 * HALF, 2 * HALF)]
            remote(part, part, h_ss.at[0], h_rs.at[zg, i], sib).wait_recv()
        hand(k, table.at[c, zg, 1 - hy])

    def group_of(k):
        step = jnp.where(k == 1, sg, jnp.where(k == 2, -sg, jnp.where(k == 3, 2, 0)))
        return lax.rem(zh + step + 4, 4)

    def absorb(k):
        zg = group_of(k)
        other = table.at[1 - c, zg]
        remote(other, other, d_ss.at[0], d_rs.at[zg], sib).wait_recv()
        keys = table[0, zg].reshape(GROUP, HD)
        far = dot_t(keys, qm[0:RL, :])
        best = jnp.max(far, axis=0, keepdims=True)
        mx[zg, :, 0:RL] = best
        far = jnp.exp2((far - best) * (inv * LOG2E))
        sm[zg, :, 0:RL] = jnp.sum(far, axis=0, keepdims=True)
        S[zg, :, 0:RL] = far
        row = lax.broadcasted_iota(jnp.int32, (GROUP, 2 * PROWS), 0)
        lane = lax.broadcasted_iota(jnp.int32, (GROUP, 2 * PROWS), 1)
        place = ((row // HALF) % NX) * GROUP + zg * 128 + (row // 256) * HALF + row % HALF
        own = dot_t(keys, qm[RL:LANES, :])
        own = jnp.where(place <= s * PROWS + lane % PROWS, own, NEG)
        best = jnp.max(own, axis=0, keepdims=True)
        mx[zg, :, RL:LANES] = best
        own = jnp.exp2((own - best) * (inv * LOG2E))
        sm[zg, :, RL:LANES] = jnp.sum(own, axis=0, keepdims=True)
        S[zg, :, RL:LANES] = own
        DP[zg] = dot_t(table[1, zg].reshape(GROUP, HD), gm[...]) - delta

    def absorb_loop(k, _):
        absorb(k)
        return 0

    take_near()
    take_far(1)
    absorb(0)
    take_far(2)
    take_far(3)
    for k in range(1, 16):
        pt = wrap(p + k, 16)
        remote(rsend.at[pt // 4], rtab.at[p], q_ss.at[0], q_rs.at[0], (pt, s)).start()
    take_beside(1)
    take_beside(2)
    take_beside(3)
    lax.fori_loop(1, 4, absorb_loop, 0)
    part = rtab.at[pl.ds(0, 15)]
    remote(part, part, q_ss.at[0], q_rs.at[0], sib).wait_recv()
    for i in range(16):
        kr[i * 16 : (i + 1) * 16, :] = rtab[i, 0:16, :]
        vr[i * 16 : (i + 1) * 16, :] = rtab[i, 16:32, :]
    u = lax.broadcasted_iota(jnp.int32, (RESP, RESP), 0)
    t = lax.broadcasted_iota(jnp.int32, (RESP, RESP), 1)
    near = (u <= t) & (u < length)
    sr = dot_t(kr[...], qm[0:RL, :])
    tops, sums = [], []
    for h in range(2):
        part = jnp.where(near, sr[:, h * RESP : (h + 1) * RESP], NEG)
        best = jnp.max(part, axis=0, keepdims=True)
        part = jnp.exp2((part - best) * (inv * LOG2E))
        Sr[:, h * RESP : (h + 1) * RESP] = part
        tops.append(best)
        sums.append(jnp.sum(part, axis=0, keepdims=True))
    tops = jnp.concatenate(tops + [jnp.full((1, 2 * PROWS), NEG, F32)], axis=1)
    sums = jnp.concatenate(sums + [jnp.zeros((1, 2 * PROWS), F32)], axis=1)


    top = tops
    for zg in range(4):
        top = jnp.maximum(top, mx[zg])
    rscale = jnp.exp2((tops - top) * (inv * LOG2E))
    total = sums * rscale
    scales = []
    for zg in range(4):
        scale = jnp.exp2((mx[zg] - top) * (inv * LOG2E))
        total += sm[zg] * scale
        scales.append(scale)
    rtotal = 1.0 / total
    rscale = rscale * rtotal
    for zg in range(4):
        mx[zg] = scales[zg] * rtotal

    prob = Sr[...] * rscale[:, 0:RL]
    dp = dot_t(vr[...], gm[0:RL, :])
    ds = (prob * (dp - delta[:, 0:RL])).astype(BF)
    dqt[:, 0:RL] = dot_l(kr[...], ds)
    dqt[:, RL:LANES] = jnp.zeros((HD, 2 * PROWS), F32)
    dkr = (dot_n(ds, qm[0:RL, :]) * inv).astype(BF)
    dvr = dot_n(prob.astype(BF), gm[0:RL, :]).astype(BF)
    for i in range(16):
        rgs[i, 0:16, :] = dkr[i * 16 : (i + 1) * 16, :]
        rgs[i, 16:32, :] = dvr[i * 16 : (i + 1) * 16, :]
    for k in range(1, 16):
        pt = wrap(p + k, 16)
        remote(rgs.at[pt], rgr.at[p], g_ss.at[0], g_rs.at[0], (pt, s)).start()
    rgr[p] = rgs[p]

    def pair(zg, kv, i):
        rows = pl.ds(pl.multiple_of((2 * i + 1 - c) * 128, 128), 128)
        got = r1.at[kv, zg, pl.ds(i * 128, 128)]
        return remote(gout.at[kv, zg, rows], got, e_ss.at[0], e_rs.at[zg], sib)

    def ysend(zg, d):
        yt = wrap(y + d, NY)
        rows = pl.ds(pl.multiple_of(zg * 32, 32), 32)
        return remote(ady.at[yt, rows], ray.at[d, rows], ya_ss.at[0], ya_rs.at[0], dev(x, yt, z, c))

    def zsend(zt):
        return remote(adz.at[zt], raz.at[z], za_ss.at[0], za_rs.at[0], dev(x, y, zt, c))

    def spread(k):
        zg = group_of(k)
        part = gout.at[0, zg]
        remote(part, part, e_ss.at[0], e_rs.at[zg], sib).wait_recv()
        for i in range(2):
            zt = zg * 2 + i
            keep = pl.ds(pl.multiple_of((2 * i + c) * 128, 128), 128)
            got = pl.ds(i * 128, 128)
            both = gout[0, zg, keep, :].astype(F32) + r1[0, zg, got, :].astype(F32)
            both = both.astype(BF)
            rows = pl.ds(pl.multiple_of(zt * 16, 16), 16)
            for yy in range(NY):
                ady[yy, rows, :] = both[yy * 16 : (yy + 1) * 16, :]
            both = gout[1, zg, keep, :].astype(F32) + r1[1, zg, got, :].astype(F32)
            adz[zt] = both.astype(BF)
        for d in (4, 3, 5, 2, 6, 1, 7):
            ysend(zg, d).start()
        for i in range(2):
            zt = zg * 2 + i

            @pl.when(zt != z)
            def _():
                zsend(zt).start()

    def grads(k, _):
        zg = group_of(k)
        prob = S[zg] * mx[zg]
        ds = (prob * DP[zg]).astype(BF)
        dqt[...] += dot_l(table[0, zg].reshape(GROUP, HD), ds)
        for kv in range(2):
            if kv == 0:
                sums = (dot_n(ds, qm[...]) * inv).astype(BF)
            else:
                sums = dot_n(prob.astype(BF), gm[...]).astype(BF)
            for half in range(2):
                for xs in range(NX):
                    start = half * 256 + xs * HALF
                    to = xs * 128 + half * HALF
                    gout[kv, zg, to : to + HALF, :] = sums[start : start + HALF, :]
        for kv in range(2):
            for i in range(2):
                pair(zg, kv, i).start()

        if k > 0:
            spread(k - 1)

        return 0

    for k in range(4):
        grads(k, 0)

    dqs = (dqt[...].T * inv).astype(BF)
    for h in range(2):
        o_rdq[0, :, h * HD : (h + 1) * HD] = dqs[h * RESP : (h + 1) * RESP, :]
        o_dq[:, h * HD : (h + 1) * HD] = dqs[RL + h * PROWS : RL + (h + 1) * PROWS, :]

    spread(3)
    seven = ray.at[pl.ds(1, 7)]
    remote(seven, seven, ya_ss.at[0], ya_rs.at[0], sib).wait_recv()
    acc = ady[y].astype(F32)
    for d in range(1, 8):
        acc += ray[d].astype(F32)
    bdy[...] = acc.astype(BF)
    for d in range(1, 8):
        zt = wrap(z + d, NZ)
        cp = remote(
            bdy.at[pl.ds(pl.multiple_of(zt * 16, 16), 16)], rbz.at[d], zb_ss.at[0], zb_rs.at[0], dev(x, y, zt, c)
        )
        cp.start()
    remote(seven, seven, za_ss.at[0], za_rs.at[0], sib).wait_recv()
    acc = adz[z].astype(F32)
    for d in range(1, 8):
        acc += raz[wrap(z + d, NZ)].astype(F32)
    bdz[...] = acc.astype(BF)
    for d in range(1, 8):
        yt = wrap(y + d, NY)
        cp = remote(
            bdz.at[pl.ds(pl.multiple_of(yt * 16, 16), 16)], rby.at[d], yb_ss.at[0], yb_rs.at[0], dev(x, yt, z, c)
        )
        cp.start()
    some = rbz.at[pl.ds(1, 7)]
    remote(some, some, zb_ss.at[0], zb_rs.at[0], sib).wait_recv()
    acc = bdy[pl.ds(pl.multiple_of(z * 16, 16), 16), :].astype(F32)
    for d in range(1, 8):
        acc += rbz[d].astype(F32)
    fin[0:16, :] = acc.astype(BF)
    remote(some, some, yb_ss.at[0], yb_rs.at[0], sib).wait_recv()
    acc = bdz[pl.ds(pl.multiple_of(y * 16, 16), 16), :].astype(F32)
    for d in range(1, 8):
        acc += rby[d].astype(F32)
    fin[16:32, :] = acc.astype(BF)

    xo = 2 * zl + c
    zf, cf = x // 2, x % 2

    def final(i):
        zz, cc = i // 2, i % 2
        same = (xo == x) & (zl == zz) & (c == cc)
        return same, remote(fin, rfin.at[x], f_ss.at[i], f_rs.at[x], dev(xo, y, zh * 2 + zz, cc))

    for i in range(4):
        same, cp = final(i)

        @pl.when(jnp.logical_not(same))
        def _():
            cp.start()

        @pl.when(same)
        def _():
            rfin[x] = fin[...]

    part = rgr.at[pl.ds(0, 15)]
    remote(part, part, g_ss.at[0], g_rs.at[0], sib).wait_recv()
    for g in range(NX):
        acc = rgr[g * 4].astype(F32)
        for i in range(1, 4):
            acc += rgr[g * 4 + i].astype(F32)
        acc = acc.astype(BF)
        o_rdk[0, :, g * HD : (g + 1) * HD] = acc[0:16, :]
        o_rdv[0, :, g * HD : (g + 1) * HD] = acc[16:32, :]

    for xs in range(NX):
        mine = (x == xs) & (zf == zl) & (cf == c)

        @pl.when(jnp.logical_not(mine))
        def _():
            remote(fin, rfin.at[xs], f_ss.at[0], f_rs.at[xs], sib).wait_recv()

    spot = zl * 2 + c
    for xs in range(NX):
        tile = rfin[xs].astype(F32)
        for half, out in ((0, o_dk), (16, o_dv)):
            rows = tile[half : half + 4, :]
            for i in range(1, 4):
                rows = jnp.where(spot == i, tile[half + 4 * i : half + 4 * i + 4, :], rows)
            out[:, xs * HD : (xs + 1) * HD] = rows.astype(BF)

    for i in range(4):
        same, cp = final(i)

        @pl.when(jnp.logical_not(same))
        def _():
            cp.wait_send()

    def sent(part, sem):
        remote(part, part, sem.at[0], p_rs.at[0, 0], sib).wait_send()

    sent(gout.at[0, pl.ds(0, 3), pl.ds(0, 384)], p_ss)
    sent(rtab.at[pl.ds(0, 15)], q_ss)
    sent(gout.at[0, pl.ds(0, 3), pl.ds(0, 256)], h_ss)
    sent(table.at[0], d_ss)
    sent(gout.at[0], e_ss)
    sent(seven, ya_ss)
    sent(seven, za_ss)
    sent(some, yb_ss)
    sent(some, zb_ss)
    sent(rtab.at[pl.ds(0, 15)], g_ss)


def place(*refs):
    for i in range(6):
        refs[6 + i][...] = refs[i][...]


def shards(*args):
    hbm = pl.BlockSpec(memory_space=pltpu.HBM)
    vmem = pl.BlockSpec(memory_space=pltpu.VMEM)
    dma = pltpu.SemaphoreType.DMA
    shape = jax.ShapeDtypeStruct
    made = pl.pallas_call(
        kernel,
        out_shape=(
            pltpu.VMEM((PROWS, 256), BF),
            pltpu.VMEM((4, 512), BF),
            pltpu.VMEM((4, 512), BF),
            pltpu.VMEM((1, RESP, 256), BF),
            pltpu.VMEM((1, 16, 512), BF),
            pltpu.VMEM((1, 16, 512), BF),
        ),
        in_specs=[hbm] * 13,
        out_specs=[vmem] * 6,
        scratch_shapes=[
            pltpu.VMEM((LANES, HD), BF),
            pltpu.VMEM((LANES, HD), BF),
            pltpu.VMEM((LANES, HD), BF),
            pltpu.VMEM((128, 512), BF),
            pltpu.VMEM((4, 128, HD), BF),
            pltpu.VMEM((2, 4, 2, GROUP // 2, HD), BF),
            pltpu.VMEM((4, 32, HD), BF),
            pltpu.VMEM((16, 32, HD), BF),
            pltpu.VMEM((RESP, HD), BF),
            pltpu.VMEM((RESP, HD), BF),
            pltpu.VMEM((4, GROUP, LANES), F32),
            pltpu.VMEM((4, GROUP, LANES), F32),
            pltpu.VMEM((RESP, RL), F32),
            pltpu.VMEM((HD, LANES), F32),
            pltpu.VMEM((4, 1, LANES), F32),
            pltpu.VMEM((4, 1, LANES), F32),
            pltpu.VMEM((2, 4, GROUP, HD), BF),
            pltpu.VMEM((2, 4, 256, HD), BF),
            pltpu.VMEM((8, 128, HD), BF),
            pltpu.VMEM((8, 128, HD), BF),
            pltpu.VMEM((8, 128, HD), BF),
            pltpu.VMEM((8, 128, HD), BF),
            pltpu.VMEM((128, HD), BF),
            pltpu.VMEM((128, HD), BF),
            pltpu.VMEM((8, 16, HD), BF),
            pltpu.VMEM((8, 16, HD), BF),
            pltpu.VMEM((32, HD), BF),
            pltpu.VMEM((4, 32, HD), BF),
            pltpu.VMEM((16, 32, HD), BF),
            pltpu.VMEM((16, 32, HD), BF),
            pltpu.SMEM((4, 4), F32),
            pltpu.SMEM((1,), jnp.int32),
            dma((7,)),
            dma((1,)),
            dma((5, 2)),
            dma((1,)),
            dma((1,)),
            dma((1,)),
            dma((4, 2)),
            dma((1,)),
            dma((4,)),
            dma((1,)),
            dma((4,)),
        ]
        + [dma((1,))] * 8
        + [dma((4,)), dma((4,)), dma((1,)), dma((1,))],
        compiler_params=pltpu.CompilerParams(
            collective_id=0, has_side_effects=True, vmem_limit_bytes=61440 * 1024
        ),
        name="attention_backward",
    )(*args)
    return pl.pallas_call(
        place,
        out_shape=tuple(shape(a.shape, BF) for a in made),
        in_specs=[vmem] * 6,
        out_specs=[vmem] * 6,
        compiler_params=pltpu.CompilerParams(vmem_limit_bytes=40 * 1024 * 1024),
        name="place_outputs",
    )(*made)


def solution(mesh):
    wide = P("sample", "prompt")
    block = P("prompt", None)
    resp = P("sample", None, "prompt")
    near = P("sample", "prompt", None)
    owned = P(("prompt", "sample"), None)
    return jax.shard_map(
        shards,
        mesh=mesh,
        in_specs=(wide, wide, wide, block, block, block, block, resp, resp, resp, near, near, P("sample")),
        out_specs=(wide, owned, owned, resp, near, near),
        check_vma=False,
    )
```
